256 devices in a mesh: gy: 32 (over y, z), gx: 8 (over x, core).
Axes of the slice: x: 4, y: 4, z: 8, core: 2. Of those that a mesh axis runs over, the one named last changes fastest.
Arguments:
- spatial_grad: float32 [3, 256, 128, 128], P(None, 'gy', 'gx'), may hold values from -4 to 4
- temporal_grad: float32 [256, 128, 128], P('gy', 'gx'), may hold values from -6 to 6
Outputs:
- flow: float32 [3, 256, 128, 128], P(None, 'gy', 'gx')
The draws below stay inside these ranges and needn't reach their ends.
All inputs are finite; a program needn't handle non-finite values.
Results may differ from the reference program's by a relative error of at most 0.0001.
Values sent between devices are 32-bit elements; how exact they have to be, the bound alone decides.
A program may use at most 192 MiB of HBM per device.

```python
import jax
import jax.numpy as jnp
from jax import lax

NZ = 128
CYCLES = 2
SMOOTH = 2
COARSE_SWEEPS = 8
NY = 256
NX = 128


def shard_levels(rng, extent, shards, smallest, high):
    def one(position, blocks):
        draws = jax.random.uniform(jax.random.fold_in(jax.random.fold_in(rng, 6), position), (blocks,), jnp.float32, smallest / len(shards), high / len(shards))
        return jnp.repeat(jnp.exp(draws), extent[position] // blocks).reshape((-1,) + (1,) * (len(extent) - position - 1))

    gain = one(*shards[0])
    for cut in shards[1:]:
        gain = gain * one(*cut)
    return gain


def centred(own_key, shape, spread, most, shards=(), dtype=jnp.bfloat16):
    factor_of = shard_levels(own_key, shape, shards, -0.22, 0.18) if shards else 1.0
    array = jax.random.normal(own_key, shape, jnp.float32) * spread * factor_of
    return jnp.minimum(jnp.maximum(array, -most), most).astype(dtype)


def setup_inputs(seed: int = 0) -> dict:
    keys = jax.random.split(jax.random.key(seed), 3)
    return {
        "spatial_grad": centred(keys[0], (3, NY, NX, NZ), 0.5, 4.0, ((1, 32), (2, 8)), jnp.float32),
        "temporal_grad": centred(keys[1], (NY, NX, NZ), 1.0, 6.0, ((0, 32), (1, 8)), jnp.float32),
    }


damping = 0.8
smooth_weight = 1.0


def pad_all(field):
    return jnp.pad(field, ((0, 0), (1, 1), (1, 1), (1, 1)))


def sym_apply(matrix, vector):
    return jnp.stack([
        matrix[0] * vector[0] + matrix[3] * vector[1] + matrix[4] * vector[2],
        matrix[3] * vector[0] + matrix[1] * vector[1] + matrix[5] * vector[2],
        matrix[4] * vector[0] + matrix[5] * vector[1] + matrix[2] * vector[2]])


def invert(coeffs, weight):
    diag_x = coeffs[0] + 6.0 * weight
    diag_y = coeffs[1] + 6.0 * weight
    diag_z = coeffs[2] + 6.0 * weight
    off_xy = coeffs[3]
    off_xz = coeffs[4]
    off_yz = coeffs[5]
    cof_xx = diag_y * diag_z - off_yz * off_yz
    cof_yy = diag_x * diag_z - off_xz * off_xz
    cof_zz = diag_x * diag_y - off_xy * off_xy
    cof_xy = off_xz * off_yz - off_xy * diag_z
    cof_xz = off_xy * off_yz - diag_y * off_xz
    cof_yz = off_xy * off_xz - diag_x * off_yz
    determinant = diag_x * cof_xx + off_xy * cof_xy + off_xz * cof_xz
    return jnp.stack([cof_xx, cof_yy, cof_zz, cof_xy, cof_xz, cof_yz]) / determinant


def neighbours(padded):
    return (padded[:, 2:, 1:-1, 1:-1] + padded[:, :-2, 1:-1, 1:-1]
            + padded[:, 1:-1, 2:, 1:-1] + padded[:, 1:-1, :-2, 1:-1]
            + padded[:, 1:-1, 1:-1, 2:] + padded[:, 1:-1, 1:-1, :-2])


def apply_core(padded, coeffs, weight):
    center = padded[:, 1:-1, 1:-1, 1:-1]
    return sym_apply(coeffs, center) + weight * (6.0 * center - neighbours(padded))


def sweep_core(padded, coeffs, inverse, source_term, weight):
    center = padded[:, 1:-1, 1:-1, 1:-1]
    residue = source_term - apply_core(padded, coeffs, weight)
    return center + damping * sym_apply(inverse, residue)


def fold_axis(padded, along):
    length = padded.shape[along] - 2
    first = lax.slice_in_dim(padded, 0, length, 2, along)
    second = lax.slice_in_dim(padded, 1, length + 1, 2, along)
    third = lax.slice_in_dim(padded, 2, length + 2, 2, along)
    fourth = lax.slice_in_dim(padded, 3, length + 2, 2, along)
    return (first + 3.0 * second + 3.0 * third + fourth) * 0.125


def restrict_core(padded):
    return fold_axis(fold_axis(fold_axis(padded, 1), 2), 3)


def spread_axis(padded, along):
    length = padded.shape[along] - 2
    lower = lax.slice_in_dim(padded, 0, length, 1, along)
    middle = lax.slice_in_dim(padded, 1, length + 1, 1, along)
    upper = lax.slice_in_dim(padded, 2, length + 2, 1, along)
    even_part = 0.75 * middle + 0.25 * lower
    odd_part = 0.75 * middle + 0.25 * upper
    stacked = jnp.stack([even_part, odd_part], axis=along + 1)
    new_shape = list(even_part.shape)
    new_shape[along] = 2 * length
    return stacked.reshape(new_shape)


def prolong_core(padded):
    return spread_axis(spread_axis(spread_axis(padded, 1), 2), 3)


def coarsen(coeffs):
    dims = coeffs.shape
    folded = coeffs.reshape(dims[0], dims[1] // 2, 2, dims[2] // 2, 2, dims[3] // 2, 2)
    return jnp.mean(folded, axis=(2, 4, 6))


def reference(spatial_grad, temporal_grad):
    grads = spatial_grad
    coeffs = [jnp.stack([grads[0] * grads[0], grads[1] * grads[1], grads[2] * grads[2],
                         grads[0] * grads[1], grads[0] * grads[2], grads[1] * grads[2]])]
    source = -temporal_grad[None] * grads
    weights = [smooth_weight]
    for level_no in range(3):
        coeffs.append(coarsen(coeffs[-1]))
        weights.append(weights[-1] * 0.25)
    inverses = [invert(coeffs[level_no], weights[level_no]) for level_no in range(4)]

    def smooth(field, level_no, source_term):
        for sweep_no in range(SMOOTH):
            field = sweep_core(pad_all(field), coeffs[level_no], inverses[level_no], source_term, weights[level_no])
        return field

    def run_cycle(field, source_term, level_no):
        if level_no == 3:
            correction = jnp.zeros_like(source_term)
            for sweep_no in range(COARSE_SWEEPS):
                correction = sweep_core(pad_all(correction), coeffs[3], inverses[3], source_term, weights[3])
            return correction
        field = smooth(field, level_no, source_term)
        residue = source_term - apply_core(pad_all(field), coeffs[level_no], weights[level_no])
        coarse_source = restrict_core(pad_all(residue))
        correction = run_cycle(jnp.zeros_like(coarse_source), coarse_source, level_no + 1)
        field = field + prolong_core(pad_all(correction))
        return smooth(field, level_no, source_term)

    field = jnp.zeros_like(source)
    for cycle_no in range(CYCLES):
        field = run_cycle(field, source, 0)
    return field
```

```python
import functools

import jax
import jax.numpy as jnp
from jax import lax
from jax.experimental import pallas as pl
from jax.experimental.pallas import tpu as pltpu
from jax.sharding import PartitionSpec as P

MESH = pl.DeviceIdType.MESH
F32 = jnp.float32
BF16 = jnp.bfloat16
KEEP = 0.2
DAMP = 0.8
W = (1.0, 0.25, 0.0625, 0.015625)

NEAR = [(a, b) for a in (-1, 0, 1) for b in (-1, 0, 1) if (a, b) != (0, 0)]
OUTER = [(a, b) for a in (-2, 2) for b in (-1, 0, 1)]
BOX = NEAR + OUTER
RING4 = [1, -1, 2, -2, 3, -3, 4, -4]
RING11 = [s * d for d in range(1, 12) for s in (1, -1)]


def loop(first, last, body):
    def step(i, carry):
        body(i)
        return carry

    lax.fori_loop(first, last, step, 0)


def iota(shape, dim):
    return lax.broadcasted_iota(jnp.int32, shape, dim)


def roll(x, shift, axis):
    return pltpu.roll(x, shift % x.shape[axis], axis)


def split_dot(x, matrix):
    high = x.astype(BF16).astype(F32)
    both = jnp.concatenate([high, x - high], axis=0).astype(BF16)
    out = jnp.dot(both, matrix, preferred_element_type=F32)
    rows = x.shape[0]
    return out[:rows] + out[rows:]


def fold_weight(d):
    return jnp.where((d == 0) | (d == 1), 3.0, jnp.where((d == -1) | (d == 2), 1.0, 0.0))


def spread_weight(d):
    return jnp.where((d == 0) | (d == 1), 0.75, jnp.where((d == -1) | (d == 2), 0.25, 0.0))


def sym(m, v):
    return [
        m[0] * v[0] + m[3] * v[1] + m[4] * v[2],
        m[3] * v[0] + m[1] * v[1] + m[5] * v[2],
        m[4] * v[0] + m[5] * v[1] + m[2] * v[2],
    ]


def damped_inverse(m, weight, mask):
    dx, dy, dz = (m[k] + 6.0 * weight for k in range(3))
    xy, xz, yz = m[3], m[4], m[5]
    cof = [
        dy * dz - yz * yz,
        dx * dz - xz * xz,
        dx * dy - xy * xy,
        xz * yz - xy * dz,
        xy * yz - dy * xz,
        xy * xz - dx * yz,
    ]
    det = dx * cof[0] + xy * cof[3] + xz * cof[4]
    scale = mask * DAMP / det
    return [c * scale for c in cof]


def kernel(
    sg, tg, out,
    IN, Q, VA, VB, R0, XM0, FS, CZ, TMP,
    RA1, A1, I1, RS1, S1, V1A, V1B, R1, XM1,
    C1, C2, F, XA, A2, I2, XG, S2, V2A, V2B, YM2, E21, P21,
    RA3, I3, SG, V3, E3, P3,
    M01, M12, M23, P01, P12, P23, M32, M21, M10,
    lsem, ssem, rsem,
):
    gy = lax.axis_index("gy")
    gx = lax.axis_index("gx")

    def at(dy, dx):
        return lax.rem(gy + dy + 32, 32), lax.rem(gx + dx + 8, 8)

    barrier = pltpu.get_barrier_semaphore()
    everyone = BOX + [(d, 0) for d in RING11 if abs(d) > 2] + [(0, d) for d in (2, 3, 4, 5, 6)]
    for peer in everyone:
        pl.semaphore_signal(barrier, inc=1, device_id=at(*peer), device_id_type=MESH)

    load_g = pltpu.make_async_copy(sg, IN.at[0:3, 7:15, 8:24], lsem.at[0])
    load_t = pltpu.make_async_copy(tg, IN.at[3, 7:15, 8:24], lsem.at[1])
    load_g.start()
    load_t.start()

    count = [0]

    def send(src, dst, peer):
        k = count[0]
        count[0] += 1
        copy = pltpu.make_async_remote_copy(
            src_ref=src, dst_ref=dst, send_sem=ssem.at[k], recv_sem=rsem.at[k],
            device_id=at(*peer), device_id_type=MESH,
        )
        copy.start()
        return copy

    def received(copies):
        for copy in copies:
            copy.wait_recv()

    sent = []

    def lanes(shape):
        return iota(shape, 0), iota(shape, 1)

    k, n = lanes((128, 128))
    M01[...] = (fold_weight(k - 2 * (n & 63)) * (1.0 / 512.0)).astype(BF16)
    P01[...] = jnp.where((k >> 1) == (n & 63), 0.125, 0.0).astype(BF16)
    M12[...] = jnp.where(k < 64, fold_weight(k - 2 * (n & 31)) * (1.0 / 512.0), 0.0).astype(BF16)
    P12[...] = jnp.where((k < 64) & ((k >> 1) == (n & 31)), 0.125, 0.0).astype(BF16)
    part = (n & 31) >> 4
    M23[...] = jnp.where(
        (k >> 5) == 2 * part, fold_weight((k & 31) - 2 * (n & 15)) * (1.0 / 512.0), 0.0
    ).astype(BF16)
    P23[...] = jnp.where(((k >> 6) == part) & (((k & 31) >> 1) == (n & 15)), 0.125, 0.0).astype(BF16)
    M10[...] = jnp.where(k < 64, spread_weight(n - 2 * k), 0.0).astype(BF16)
    for q in range(4):
        M21[:, 128 * q:128 * q + 128] = jnp.where(
            ((k >> 5) == q) & (n < 64), spread_weight(n - 2 * (k & 31)), 0.0
        ).astype(BF16)
        for eo in range(2):
            xs = n >> 5
            fits = ((xs & 1) == eo) & ((k >> 4) == 2 * q + (xs >> 1))
            M32[eo, :, 128 * q:128 * q + 128] = jnp.where(
                fits, spread_weight((n & 31) - 2 * (k & 15)), 0.0
            ).astype(BF16)

    row = iota((32, 128), 0) + (16 * gx - 8)
    XM0[...] = jnp.where((row >= 0) & (row < 128), 1.0, 0.0)
    row = iota((24, 128), 0) + (8 * gx - 8)
    XM1[...] = jnp.where((row >= 0) & (row < 64) & (iota((24, 128), 1) < 64), 1.0, 0.0)
    plane = iota((18, 8, 128), 0) + (2 * gy - 8)
    YM2[...] = jnp.where((plane >= 0) & (plane < 64), 1.0, 0.0)
    E21[...] = jnp.zeros_like(E21)
    SG[:, 0:8] = jnp.zeros((2, 8, 128), F32)
    RA3[0:16] = jnp.zeros((16, 128), F32)

    def ym(first, length, y):
        place = first + y
        return jnp.where((place >= 0) & (place < length), 1.0, 0.0).astype(F32)

    def ym0(y):
        return ym(8 * gy - 7, 256, y)

    def ym1(y):
        return ym(4 * gy - 8, 128, y)

    def pack(rows, group):
        size = rows.shape[0]
        keep = (iota(rows.shape, 1) >> 5) == (iota(rows.shape, 0) & 3)
        F[0:size] = jnp.where(keep, rows, 0.0)
        kept = 8 * ((size // group + 7) // 8)
        total = F[pl.ds(0, kept, stride=group)]
        for r in range(1, group):
            total = total + F[pl.ds(r, kept, stride=group)]
        return total

    F[...] = jnp.zeros_like(F)

    load_g.wait()
    load_t.wait()

    def own_coeffs(i):
        def products(y):
            g = [IN[c, y, 8:24] for c in range(3)]
            return [g[0] * g[0], g[1] * g[1], g[2] * g[2], g[0] * g[1], g[0] * g[2], g[1] * g[2]]

        one, two = products(7 + 2 * i), products(8 + 2 * i)
        for f in range(6):
            FS[f, 0:16] = one[f] + two[f]
        for f in range(6):
            C1[pl.ds(f * 32 + 8 * i, 8)] = FS[f, pl.ds(0, 8, stride=2)] + FS[f, pl.ds(1, 8, stride=2)]

    loop(0, 4, own_coeffs)
    C2[...] = split_dot(C1[...], P01[...])
    low = iota((8, 128), 1) < 64
    for f in range(6):
        for j in range(2):
            RA1[2, 1, f, j] = jnp.where(
                low, C2[32 * f + 8 * j:32 * f + 8 * j + 8], C2[32 * f + 8 * j + 16:32 * f + 8 * j + 24]
            )
    halved = C2[pl.ds(0, 96, stride=2)] + C2[pl.ds(1, 96, stride=2)]
    XA[pl.ds(pl.multiple_of(gx * 16, 16), 16)] = pack(split_dot(halved, P12[...]), 8)

    pl.semaphore_wait(barrier, len(everyone))

    span = {-1: (0, 8, 24), 0: (0, 16, 8), 1: (8, 8, 0)}

    def input_copy(peer, rows):
        dy, dx = peer
        x0, width, to = span[dx]
        if dy == 0:
            y0, height, y1 = 0, 8, 7
        elif rows == "near":
            height = 3
            y0, y1 = (5, 4) if dy == 1 else (0, 15)
        else:
            height = 4
            y0, y1 = (1, 0) if dy == 1 else (3, 18)
        return send(
            IN.at[:, 7 + y0:7 + y0 + height, 8 + x0:8 + x0 + width],
            IN.at[:, y1:y1 + height, to:to + width],
            peer,
        )

    near_in = [input_copy(peer, "near") for peer in NEAR]
    a2_x = [
        send(XA.at[pl.ds(pl.multiple_of(gx * 16, 16), 16)], XA.at[pl.ds(pl.multiple_of(gx * 16, 16), 16)], (0, d))
        for d in range(1, 8)
    ]
    a1_in = {peer: send(RA1.at[2, 1], RA1.at[2 - peer[0], 1 - peer[1]], peer) for peer in BOX}
    far_in = [input_copy(peer, "far") for peer in NEAR if peer[0] != 0]
    sent += near_in + a2_x + list(a1_in.values()) + far_in
    received(near_in)

    lane0 = iota((32, 128), 1)
    first_lane, last_lane = lane0 == 0, lane0 == 127

    def around0(src, y):
        centre, total = [], []
        for c in range(3):
            v = src[c, y]
            n = src[c, y - 1] + src[c, y + 1]
            n = n + (roll(v, 1, 0) + roll(v, -1, 0))
            n = n + jnp.where(first_lane, 0.0, roll(v, 1, 1)) + jnp.where(last_lane, 0.0, roll(v, -1, 1))
            centre.append(v)
            total.append(n)
        return centre, total

    def dot3(a, b):
        return a[0] * b[0] + a[1] * b[1] + a[2] * b[2]

    def start0(y):
        g = [IN[c, y] for c in range(3)]
        q = XM0[...] * ym0(y) * (DAMP / 6.0) / (6.0 + dot3(g, g))
        Q[y] = q
        scale = -6.0 * IN[3, y] * q
        for c in range(3):
            VA[c, y] = scale * g[c]

    def swept0(src, y):
        g = [IN[c, y] for c in range(3)]
        t = IN[3, y]
        v, n = around0(src, y)
        p = [n[c] - t * g[c] for c in range(3)]
        d = dot3(g, p) * Q[y]
        scale = XM0[...] * (ym0(y) * (DAMP / 6.0))
        return [KEEP * v[c] + scale * p[c] - d * g[c] for c in range(3)]

    def sweep0(src, dst, first, last):
        def body(y):
            new = swept0(src, y)
            for c in range(3):
                dst[c, y] = new[c]

        loop(first, last, body)

    def residue0(src):
        def body(y):
            g = [IN[c, y] for c in range(3)]
            v, n = around0(src, y)
            d = IN[3, y] + dot3(g, v)
            m = XM0[...] * ym0(y)
            for c in range(3):
                R0[c, y - 6] = m * (n[c] - 6.0 * v[c] - g[c] * d)

        loop(6, 16, body)

    def fold_rows(src, c, y, x, size):
        weights = (1.0, 3.0, 3.0, 1.0)
        total = None
        for kx in range(4):
            line = None
            for ky in range(4):
                term = src[c, y + ky, pl.ds(x + kx, size, stride=2)]
                term = term if weights[ky] == 1.0 else weights[ky] * term
                line = term if line is None else line + term
            line = line if weights[kx] == 1.0 else weights[kx] * line
            total = line if total is None else total + line
        return total

    def source1(cycle):
        def body(i):
            for c in range(3):
                C1[pl.ds(c * 32 + 8 * i, 8)] = fold_rows(R0, c, 2 * i, 7, 8)

        loop(0, 4, body)
        s = split_dot(C1[0:96], M01[...])
        for c in range(3):
            for j in range(2):
                at0 = 32 * c + 8 * j
                RS1[cycle, 2, 1, c, j] = jnp.where(low, s[at0:at0 + 8], s[at0 + 16:at0 + 24])

    low4 = iota((3, 2, 8, 128), 3) < 64
    low6 = iota((6, 2, 8, 128), 3) < 64

    def unpack(src, dst, mask, group):
        for dx in range(3):
            p = src[group, dx]
            other = pltpu.roll(p.reshape(-1, 128), 64, 1).reshape(p.shape)
            dst[:, pl.ds(4 * group, 2), 8 * dx:8 * dx + 8] = jnp.where(mask, p, 0.0)
            dst[:, pl.ds(4 * group + 2, 2), 8 * dx:8 * dx + 8] = jnp.where(mask, other, 0.0)

    def inverse1(y):
        m = damped_inverse([A1[f, y] for f in range(6)], W[1], XM1[...] * ym1(y))
        for f in range(6):
            I1[f, y] = m[f]

    def around1(src, y):
        centre, total = [], []
        for c in range(3):
            v = src[c, y]
            n = src[c, y - 1] + src[c, y + 1]
            n = n + (roll(v, 1, 0) + roll(v, -1, 0)) + (roll(v, 1, 1) + roll(v, -1, 1))
            centre.append(v)
            total.append(n)
        return centre, total

    def start1(y):
        new = sym([I1[f, y] for f in range(6)], [S1[c, y] for c in range(3)])
        for c in range(3):
            V1A[c, y] = new[c]

    def sweep1(src, dst, first, last):
        def body(y):
            v, n = around1(src, y)
            new = sym([I1[f, y] for f in range(6)], [S1[c, y] + W[1] * n[c] for c in range(3)])
            for c in range(3):
                dst[c, y] = KEEP * v[c] + new[c]

        loop(first, last, body)

    def residue1(src):
        def body(y):
            v, n = around1(src, y)
            av = sym([A1[f, y] for f in range(6)], v)
            m = XM1[...] * ym1(y)
            for c in range(3):
                R1[c, y - 7] = m * (S1[c, y] + W[1] * (n[c] - 6.0 * v[c]) - av[c])

        loop(7, 13, body)

    def source2(cycle):
        rows = []
        for c in range(3):
            for i in range(2):
                FS[0, 4 * (2 * c + i):4 * (2 * c + i) + 4] = fold_rows(R1, c, 2 * i, 7, 4)
        XG[cycle, pl.ds(pl.multiple_of(gx * 8, 8), 8)] = pack(split_dot(FS[0, 0:24], M12[...]), 4)

    def shifts2(v):
        lane, r = iota(v.shape, 1), iota(v.shape, 0) & 7
        up = roll(v, -32, 1)
        xp = jnp.where(lane < 96, up, jnp.where(r == 7, 0.0, roll(up, -1, 0)))
        down = roll(v, 32, 1)
        xm = jnp.where(lane >= 32, down, jnp.where(r == 0, 0.0, roll(down, 1, 0)))
        return xm, xp

    def around2(src, first, last):
        centre, total = [], []
        for c in range(3):
            v3 = src[c, first:last]
            v = v3.reshape(-1, 128)
            z = iota(v.shape, 1) & 31
            xm, xp = shifts2(v)
            n = xm + xp + jnp.where(z == 0, 0.0, roll(v, 1, 1)) + jnp.where(z == 31, 0.0, roll(v, -1, 1))
            n = n.reshape(v3.shape) + (src[c, first - 1:last - 1] + src[c, first + 1:last + 1])
            centre.append(v3)
            total.append(n)
        return centre, total

    def start2(cycle, first, last):
        new = sym([I2[f, first:last] for f in range(6)], [S2[cycle, c, first:last] for c in range(3)])
        for c in range(3):
            V2A[c, first:last] = new[c]

    def sweep2(cycle, src, dst, first, last):
        v, n = around2(src, first, last)
        p = [S2[cycle, c, first:last] + W[2] * n[c] for c in range(3)]
        new = sym([I2[f, first:last] for f in range(6)], p)
        for c in range(3):
            dst[c, first:last] = KEEP * v[c] + new[c]

    def source3(cycle):
        v, n = around2(V2B, 7, 11)
        av = sym([A2[f, 7:11] for f in range(6)], v)
        rows = []
        for c in range(3):
            r = YM2[7:11] * (S2[cycle, c, 7:11] + W[2] * (n[c] - 6.0 * v[c]) - av[c])
            f = r[0] + 3.0 * (r[1] + r[2]) + r[3]
            xm, xp = shifts2(f)
            _, more = shifts2(3.0 * f + xp)
            rows.append(xm + 3.0 * f + more)
        SG[cycle, 96:104] = pack(split_dot(jnp.concatenate(rows, axis=0), M23[...]), 4)

    lane3 = iota((24, 128), 1)

    def shifts3(a, b):
        ua, ub = roll(a, -16, 1), roll(b, -16, 1)
        da, db = roll(a, 16, 1), roll(b, 16, 1)
        up = jnp.where(lane3 < 112, ua, ub), jnp.where(lane3 < 112, ub, 0.0)
        down = jnp.where(lane3 >= 16, da, 0.0), jnp.where(lane3 >= 16, db, da)
        return down, up

    def solve3(cycle):
        s = [[SG[cycle, pl.ds(2 * c + h, 24, stride=8)] for h in range(2)] for c in range(3)]
        for h in range(2):
            new = sym([I3[f, h] for f in range(6)], [s[c][h] for c in range(3)])
            for c in range(3):
                V3[c, h] = new[c]

        def body(i):
            v = [[V3[c, h] for h in range(2)] for c in range(3)]
            p = [[None, None] for c in range(3)]
            for c in range(3):
                down, up = shifts3(v[c][0], v[c][1])
                for h in range(2):
                    a = v[c][h]
                    n = roll(a, 1, 0) + roll(a, -1, 0) + down[h] + up[h]
                    n = n + jnp.where((lane3 & 15) == 0, 0.0, roll(a, 1, 1))
                    n = n + jnp.where((lane3 & 15) == 15, 0.0, roll(a, -1, 1))
                    p[c][h] = SG[cycle, pl.ds(2 * c + h, 24, stride=8)] + W[3] * n
            for h in range(2):
                new = sym([I3[f, h] for f in range(6)], [p[c][h] for c in range(3)])
                for c in range(3):
                    V3[c, h] = KEEP * v[c][h] + new[c]

        loop(0, 7, body)

    def spread3():
        for c in range(3):
            a, b = V3[c, 0], V3[c, 1]
            down, up = shifts3(a, b)
            for h, v in enumerate((a, b)):
                even = 0.75 * v + 0.25 * down[h]
                odd = 0.75 * v + 0.25 * up[h]
                E3[0, pl.ds(32 * c + h, 16, stride=2)] = even[8:24]
                E3[1, pl.ds(32 * c + h, 16, stride=2)] = odd[8:24]
        fine = split_dot(E3[0], M32[0]) + split_dot(E3[1], M32[1])
        for q in range(4):
            P3[pl.ds(q, 96, stride=4)] = fine[:, 128 * q:128 * q + 128]
        for c in range(3):
            def planes(i):
                return P3[128 * c + 8 * i:128 * c + 8 * i + 56].reshape(7, 8, 128)

            before, mid, after = planes(0), planes(1), planes(2)
            even = 0.75 * mid + 0.25 * before
            odd = 0.75 * mid + 0.25 * after
            for i in range(7):
                y = 2 + 2 * i
                V2B[c, y] = (V2B[c, y] + even[i]) * YM2[y]
                V2B[c, y + 1] = (V2B[c, y + 1] + odd[i]) * YM2[y + 1]

    def spread2():
        for c in range(3):
            v = V2B[c, 4:14].reshape(80, 128)
            xm, xp = shifts2(v)
            E21[0, 8 + 80 * c:88 + 80 * c] = 0.75 * v + 0.25 * xm
            E21[1, 8 + 80 * c:88 + 80 * c] = 0.75 * v + 0.25 * xp
        lines = []
        for j in range(3):
            inside = jnp.where((gx + j >= 1) & (gx + j <= 8), 1.0, 0.0).astype(F32)
            for eo in range(2):
                lines.append(E21[eo, pl.ds(7 + gx + j, 32, stride=8)] * inside)
        fine = split_dot(jnp.concatenate(lines, axis=0), M21[...])
        for j in range(3):
            for eo in range(2):
                for q in range(4):
                    at0 = 32 * (2 * j + eo)
                    P21[pl.ds(8 * j + 2 * q + eo, 32, stride=24)] = fine[at0:at0 + 32, 128 * q:128 * q + 128]

        def body(p):
            for c in range(3):
                def lines_of(i):
                    return P21[pl.ds(pl.multiple_of((10 * c + i) * 24, 8), 24)]

                mid = 0.75 * lines_of(p)
                even = mid + 0.25 * lines_of(p - 1)
                odd = mid + 0.25 * lines_of(p + 1)
                V1B[c, 2 * p] = (V1B[c, 2 * p] + even) * (XM1[...] * ym1(2 * p))
                V1B[c, 2 * p + 1] = (V1B[c, 2 * p + 1] + odd) * (XM1[...] * ym1(2 * p + 1))

        loop(1, 9, body)

    def spread1(first, last):
        for c in range(3):
            CZ[c] = split_dot(V1B[c, 4:16].reshape(288, 128), M10[...]).reshape(12, 24, 128)

        def body(p):
            for b in range(2):
                y = 2 * p - 1 + b
                m = XM0[...] * ym0(y)
                for c in range(3):
                    a = 0.75 * CZ[c, p] + 0.25 * CZ[c, p - 1 + 2 * b]
                    mid = 0.75 * roll(a, -4, 0)
                    TMP[b, c, pl.ds(0, 16, stride=2)] = (mid + 0.25 * roll(a, -3, 0))[0:16]
                    TMP[b, c, pl.ds(1, 16, stride=2)] = (mid + 0.25 * roll(a, -5, 0))[0:16]
                    VB[c, y] = (VB[c, y] + TMP[b, c]) * m

        loop(first, last, body)

    for cycle in range(2):
        if cycle == 0:
            loop(4, 18, start0)
            sweep0(VA, VB, 5, 17)
        else:
            sweep0(VB, VA, 4, 18)
            sweep0(VA, VB, 5, 17)
        residue0(VB)
        source1(cycle)
        s1 = {
            peer: send(RS1.at[cycle, 2, 1], RS1.at[cycle, 2 - peer[0], 1 - peer[1]], peer) for peer in BOX
        }
        sent += list(s1.values())

        if cycle == 0:
            received(a2_x)
            rows = []
            for f in range(6):
                one = XA[pl.ds(2 * f, 8, stride=16)]
                two = XA[pl.ds(2 * f + 1, 8, stride=16)]
                A2[f, 8] = one
                A2[f, 9] = two
                rows.append(one + two)
            RA3[192:208] = pack(split_dot(jnp.concatenate(rows, axis=0), P23[...]), 4)
            a2 = [send(A2.at[:, 8:10], A2.at[:, 8 - 2 * d:10 - 2 * d], (d, 0)) for d in RING4]
            a3 = [send(RA3.at[192:208], RA3.at[192 - 16 * d:208 - 16 * d], (d, 0)) for d in RING11]
            sent += a2 + a3
            received(a1_in.values())
            loop(0, 5, functools.partial(unpack, RA1, A1, low6))
            loop(0, 20, inverse1)

        received([s1[peer] for peer in NEAR])
        loop(1, 4, functools.partial(unpack, RS1.at[cycle], S1, low4))
        loop(5, 15, start1)
        sweep1(V1A, V1B, 6, 14)
        residue1(V1B)
        source2(cycle)
        own = pl.ds(pl.multiple_of(gx * 8, 8), 8)
        s2_x = [send(XG.at[cycle, own], XG.at[cycle, own], (0, d)) for d in range(1, 8)]
        sent += s2_x

        received([s1[peer] for peer in OUTER])
        for group in (0, 4):
            unpack(RS1.at[cycle], S1, low4, group)
        loop(1, 5, start1)
        loop(15, 19, start1)
        sweep1(V1A, V1B, 2, 6)
        sweep1(V1A, V1B, 14, 18)

        received(s2_x)
        for c in range(3):
            for j in range(2):
                S2[cycle, c, 8 + j] = XG[cycle, pl.ds(2 * c + j, 8, stride=8)]
        s2 = [send(S2.at[cycle, :, 8:10], S2.at[cycle, :, 8 - 2 * d:10 - 2 * d], (d, 0)) for d in RING4]
        sent += s2
        if cycle == 0:
            received(a2)
            m = damped_inverse([A2[f] for f in range(6)], W[2], YM2[...])
            for f in range(6):
                I2[f] = m[f]
        received(s2[:4])
        start2(cycle, 5, 13)
        sweep2(cycle, V2A, V2B, 6, 12)
        source3(cycle)
        s3 = [send(SG.at[cycle, 96:104], SG.at[cycle, 96 - 8 * d:104 - 8 * d], (d, 0)) for d in RING11]
        sent += s3

        received(s2[4:])
        start2(cycle, 1, 5)
        start2(cycle, 13, 17)
        sweep2(cycle, V2A, V2B, 2, 6)
        sweep2(cycle, V2A, V2B, 12, 16)
        if cycle == 0:
            received(far_in)
            loop(0, 4, start0)
            loop(18, 22, start0)
            sweep0(VA, VB, 1, 5)
            sweep0(VA, VB, 17, 21)
            received(a3)
            place = iota((24, 128), 0) + (gy - 12)
            mask = jnp.where((place >= 0) & (place < 32), 1.0, 0.0)
            for h in range(2):
                m = damped_inverse([RA3[pl.ds(2 * f + h, 24, stride=16)] for f in range(6)], W[3], mask)
                for f in range(6):
                    I3[f, h] = m[f]
        for copy in sent:
            copy.wait_send()
        sent = []

        received(s3)
        solve3(cycle)
        spread3()
        sweep2(cycle, V2B, V2A, 3, 15)
        sweep2(cycle, V2A, V2B, 4, 14)
        spread2()
        sweep1(V1B, V1A, 3, 17)
        sweep1(V1A, V1B, 4, 16)
        if cycle == 0:
            spread1(1, 11)
            sweep0(VB, VA, 2, 20)
            sweep0(VA, VB, 3, 19)
        else:
            spread1(3, 9)
            sweep0(VB, VA, 6, 16)

            def last(y):
                new = swept0(VA, y)
                for c in range(3):
                    out[c, y - 7] = new[c][8:24]

            loop(7, 15, last)


TRANSFERS = 8 + 7 + 14 + 6 + 8 + 22 + 2 * (14 + 7 + 8 + 22)


def local(spatial_grad, temporal_grad):
    def v(*shape, dtype=F32):
        return pltpu.VMEM(shape, dtype)

    def m(*shape):
        return pltpu.VMEM(shape, BF16)

    scratch = [
        v(4, 22, 32, 128), v(22, 32, 128), v(3, 22, 32, 128), v(3, 22, 32, 128), v(3, 10, 32, 128),
        v(32, 128), v(6, 32, 128), v(3, 12, 24, 128), v(2, 3, 32, 128),
        v(5, 3, 6, 2, 8, 128), v(6, 20, 24, 128), v(6, 20, 24, 128), v(2, 5, 3, 3, 2, 8, 128), v(3, 20, 24, 128),
        v(3, 20, 24, 128), v(3, 20, 24, 128), v(3, 6, 24, 128), v(24, 128),
        v(192, 128), v(192, 128), v(128, 128), v(128, 128), v(6, 18, 8, 128), v(6, 18, 8, 128), v(2, 64, 128),
        v(2, 3, 18, 8, 128), v(3, 18, 8, 128), v(3, 18, 8, 128), v(18, 8, 128), v(2, 272, 128), v(768, 128),
        v(384, 128), v(6, 2, 24, 128), v(2, 192, 128), v(3, 2, 24, 128), v(2, 96, 128), v(384, 128),
        m(128, 128), m(128, 128), m(128, 128), m(128, 128), m(128, 128), m(128, 128),
        m(2, 128, 512), m(128, 512), m(128, 128),
        pltpu.SemaphoreType.DMA((2,)),
        pltpu.SemaphoreType.DMA((TRANSFERS,)),
        pltpu.SemaphoreType.DMA((TRANSFERS,)),
    ]
    return pl.pallas_call(
        kernel,
        out_shape=jax.ShapeDtypeStruct(spatial_grad.shape, F32),
        in_specs=[pl.BlockSpec(memory_space=pl.ANY)] * 2,
        out_specs=pl.BlockSpec(memory_space=pltpu.VMEM),
        scratch_shapes=scratch,
        compiler_params=pltpu.CompilerParams(
            collective_id=0, has_side_effects=True, vmem_limit_bytes=48 * 2**20
        ),
        name="flow",
    )(spatial_grad, temporal_grad)


def solution(mesh):
    placed = (P(None, "gy", "gx", None), P("gy", "gx", None))
    return jax.shard_map(
        local, mesh=mesh, in_specs=placed, out_specs=P(None, "gy", "gx", None), check_vma=False
    )
```

```python
import functools

import jax
import jax.numpy as jnp
from jax import lax
from jax.experimental import pallas as pl
from jax.experimental.pallas import tpu as pltpu
from jax.sharding import PartitionSpec as P

MESH = pl.DeviceIdType.MESH
F32 = jnp.float32
BF16 = jnp.bfloat16
KEEP = 0.2
DAMP = 0.8
W = (1.0, 0.25, 0.0625, 0.015625)

NEAR = [(a, b) for a in (-1, 0, 1) for b in (-1, 0, 1) if (a, b) != (0, 0)]
OUTER = [(a, b) for a in (-2, 2) for b in (-1, 0, 1)]
BOX = NEAR + OUTER
SHEET = [(a, b) for a in (2, -2, 1, -1, 0) for b in range(8) if (a, b) != (0, 0)]
RING = [s * d for d in range(1, 12) for s in (1, -1)]


def loop(first, last, body):
    def step(i, carry):
        body(i)
        return carry

    lax.fori_loop(first, last, step, 0, unroll=4)


def iota(shape, dim):
    return lax.broadcasted_iota(jnp.int32, shape, dim)


def roll(x, shift, axis):
    return pltpu.roll(x, shift % x.shape[axis], axis)


def split_dot(x, matrix):
    high = x.astype(BF16).astype(F32)
    both = jnp.concatenate([high, x - high], axis=0).astype(BF16)
    out = jnp.dot(both, matrix, preferred_element_type=F32)
    rows = x.shape[0]
    return out[:rows] + out[rows:]


def fold_weight(d):
    return jnp.where((d == 0) | (d == 1), 3.0, jnp.where((d == -1) | (d == 2), 1.0, 0.0))


def spread_weight(d):
    return jnp.where((d == 0) | (d == 1), 0.75, jnp.where((d == -1) | (d == 2), 0.25, 0.0))


def sym(m, v):
    return [
        m[0] * v[0] + m[3] * v[1] + m[4] * v[2],
        m[3] * v[0] + m[1] * v[1] + m[5] * v[2],
        m[4] * v[0] + m[5] * v[1] + m[2] * v[2],
    ]


def damped_inverse(m, weight, mask):
    dx, dy, dz = (m[k] + 6.0 * weight for k in range(3))
    xy, xz, yz = m[3], m[4], m[5]
    cof = [
        dy * dz - yz * yz,
        dx * dz - xz * xz,
        dx * dy - xy * xy,
        xz * yz - xy * dz,
        xy * yz - dy * xz,
        xy * xz - dx * yz,
    ]
    det = dx * cof[0] + xy * cof[3] + xz * cof[4]
    scale = mask * DAMP / det
    return [c * scale for c in cof]


def kernel(
    sg, tg, out,
    IN, Q, VA, VB, R0, XM0, FS, CZ, TMP,
    RA1, A1, I1, RS1, S1, V1A, V1B, R1, XM1,
    C1, C2, F, XA, A2, I2, XG, S2, V2A, V2B, YM2, E21, P21,
    RA3, I3, SG, V3, E3, P3,
    M01, M12, M23, P01, P12, P23, M32, M21, M10,
    lsem, ssem, rsem,
):
    gy = lax.axis_index("gy")
    gx = lax.axis_index("gx")

    core = lax.rem(gx, 2)
    side = 1 - 2 * core
    twin = (0, side)

    def at(dy, dx):
        return lax.rem(gy + dy + 32, 32), lax.rem(gx + dx + 8, 8)

    barrier = pltpu.get_barrier_semaphore()
    everyone = SHEET + [(d, 0) for d in RING if abs(d) > 2]
    for peer in everyone:
        pl.semaphore_signal(barrier, inc=1, device_id=at(*peer), device_id_type=MESH)

    load_g = pltpu.make_async_copy(sg, IN.at[0:3, 7:15, 8:24], lsem.at[0])
    load_t = pltpu.make_async_copy(tg, IN.at[3, 7:15, 8:24], lsem.at[1])
    load_g.start()
    load_t.start()

    count = [0]

    def send(src, dst, peer):
        k = count[0]
        count[0] += 1
        copy = pltpu.make_async_remote_copy(
            src_ref=src, dst_ref=dst, send_sem=ssem.at[k], recv_sem=rsem.at[k],
            device_id=at(*peer), device_id_type=MESH,
        )
        copy.start()
        return copy

    def received(copies):
        for copy in copies:
            copy.wait_recv()

    sent = []

    def lanes(shape):
        return iota(shape, 0), iota(shape, 1)

    k, n = lanes((128, 128))
    M01[...] = (fold_weight(k - 2 * (n & 63)) * (1.0 / 512.0)).astype(BF16)
    P01[...] = jnp.where((k >> 1) == (n & 63), 0.125, 0.0).astype(BF16)
    M12[...] = jnp.where(k < 64, fold_weight(k - 2 * (n & 31)) * (1.0 / 512.0), 0.0).astype(BF16)
    P12[...] = jnp.where((k < 64) & ((k >> 1) == (n & 31)), 0.125, 0.0).astype(BF16)
    part = (n & 31) >> 4
    M23[...] = jnp.where(
        (k >> 5) == 2 * part, fold_weight((k & 31) - 2 * (n & 15)) * (1.0 / 512.0), 0.0
    ).astype(BF16)
    P23[...] = jnp.where(((k >> 6) == part) & (((k & 31) >> 1) == (n & 15)), 0.125, 0.0).astype(BF16)
    M10[...] = jnp.where(k < 64, spread_weight(n - 2 * k), 0.0).astype(BF16)
    for q in range(4):
        M21[:, 128 * q:128 * q + 128] = jnp.where(
            ((k >> 5) == q) & (n < 64), spread_weight(n - 2 * (k & 31)), 0.0
        ).astype(BF16)
        for eo in range(2):
            xs = n >> 5
            fits = ((xs & 1) == eo) & ((k >> 4) == 2 * q + (xs >> 1))
            M32[eo, :, 128 * q:128 * q + 128] = jnp.where(
                fits, spread_weight((n & 31) - 2 * (k & 15)), 0.0
            ).astype(BF16)

    row = iota((32, 128), 0) + (16 * gx - 8)
    XM0[...] = jnp.where((row >= 0) & (row < 128), 1.0, 0.0)
    row = iota((24, 128), 0) + (8 * gx - 8)
    XM1[...] = jnp.where((row >= 0) & (row < 64) & (iota((24, 128), 1) < 64), 1.0, 0.0)
    plane = iota((18, 8, 128), 0) + (2 * gy - 8)
    YM2[...] = jnp.where((plane >= 0) & (plane < 64), 1.0, 0.0)
    E21[...] = jnp.zeros_like(E21)
    SG[:, 0:8] = jnp.zeros((2, 8, 128), F32)
    RA3[0:16] = jnp.zeros((16, 128), F32)

    def ym(first, length, y):
        place = first + y
        return jnp.where((place >= 0) & (place < length), 1.0, 0.0).astype(F32)

    def ym0(y):
        return ym(8 * gy - 7, 256, y)

    def ym1(y):
        return ym(4 * gy - 8, 128, y)

    def pack(rows, group):
        size = rows.shape[0]
        keep = (iota(rows.shape, 1) >> 5) == (iota(rows.shape, 0) & 3)
        F[0:size] = jnp.where(keep, rows, 0.0)
        kept = 8 * ((size // group + 7) // 8)
        total = F[pl.ds(0, kept, stride=group)]
        for r in range(1, group):
            total = total + F[pl.ds(r, kept, stride=group)]
        return total

    F[...] = jnp.zeros_like(F)

    load_g.wait()
    load_t.wait()

    def own_coeffs(i):
        def products(y):
            g = [IN[c, y, 8:24] for c in range(3)]
            return [g[0] * g[0], g[1] * g[1], g[2] * g[2], g[0] * g[1], g[0] * g[2], g[1] * g[2]]

        one, two = products(7 + 2 * i), products(8 + 2 * i)
        for f in range(6):
            FS[f, 0:16] = one[f] + two[f]
        for f in range(6):
            C1[pl.ds(f * 32 + 8 * i, 8)] = FS[f, pl.ds(0, 8, stride=2)] + FS[f, pl.ds(1, 8, stride=2)]

    loop(0, 4, own_coeffs)
    C2[...] = split_dot(C1[...], P01[...])
    low = iota((8, 128), 1) < 64
    for f in range(6):
        for j in range(2):
            RA1[2, 1, f, j] = jnp.where(
                low, C2[32 * f + 8 * j:32 * f + 8 * j + 8], C2[32 * f + 8 * j + 16:32 * f + 8 * j + 24]
            )
    halved = C2[pl.ds(0, 96, stride=2)] + C2[pl.ds(1, 96, stride=2)]
    XA[pl.ds(pl.multiple_of(gx * 16, 16), 16)] = pack(split_dot(halved, P12[...]), 8)

    pl.semaphore_wait(barrier, len(everyone))

    def input_copy(peer, rows, columns):
        (y0, y1, height), (x0, x1, width) = rows, columns
        return send(
            IN.at[:, 7 + y0:7 + y0 + height, 8 + x0:8 + x0 + width],
            IN.at[:, y1:y1 + height, x1:x1 + width],
            peer,
        )

    y_near = {1: (5, 4, 3), -1: (0, 15, 3)}
    y_far = {1: (1, 0, 4), -1: (3, 18, 4)}
    x_near = {1: (13, 5, 3), -1: (0, 24, 3)}
    x_wide = {1: (9, 1, 7), -1: (0, 24, 7)}
    x_rest = {1: (9, 1, 4), -1: (3, 27, 4)}
    x_all = {1: (8, 0, 8), -1: (0, 24, 8)}

    near_in = [input_copy((dy, dx), y_near[dy], x_near[dx]) for dy in (1, -1) for dx in (1, -1)]
    near_in += [input_copy((dy, 0), y_near[dy], (0, 8, 16)) for dy in (1, -1)]
    near_in += [input_copy((0, dx), (0, 7, 8), x_all[dx]) for dx in (1, -1)]
    own_a2 = pl.ds(pl.multiple_of(gx * 16, 16), 16)
    a2_x = [send(XA.at[own_a2], XA.at[own_a2], (0, d)) for d in range(1, 8)]

    def box_copy(src, dst, peer):
        return send(src.at[2, 1], dst.at[2 - peer[0], 1 - peer[1]], peer)

    a1_near = [box_copy(RA1, RA1, peer) for peer in NEAR]
    sent += near_in + a2_x + a1_near
    received(near_in)

    lane0 = iota((32, 128), 1)
    first_lane, last_lane = lane0 == 0, lane0 == 127

    def around0(src, y):
        centre, total = [], []
        for c in range(3):
            v = src[c, y]
            n = src[c, y - 1] + src[c, y + 1]
            n = n + (roll(v, 1, 0) + roll(v, -1, 0))
            n = n + jnp.where(first_lane, 0.0, roll(v, 1, 1)) + jnp.where(last_lane, 0.0, roll(v, -1, 1))
            centre.append(v)
            total.append(n)
        return centre, total

    def dot3(a, b):
        return a[0] * b[0] + a[1] * b[1] + a[2] * b[2]

    def start0(y):
        g = [IN[c, y] for c in range(3)]
        q = XM0[...] * ym0(y) * (DAMP / 6.0) / (6.0 + dot3(g, g))
        Q[y] = q
        scale = -6.0 * IN[3, y] * q
        for c in range(3):
            VA[c, y] = scale * g[c]

    def swept0(src, y):
        g = [IN[c, y] for c in range(3)]
        t = IN[3, y]
        v, n = around0(src, y)
        p = [n[c] - t * g[c] for c in range(3)]
        d = dot3(g, p) * Q[y]
        scale = XM0[...] * (ym0(y) * (DAMP / 6.0))
        return [KEEP * v[c] + scale * p[c] - d * g[c] for c in range(3)]

    def sweep0(src, dst, first, last):
        def body(y):
            new = swept0(src, y)
            for c in range(3):
                dst[c, y] = new[c]

        loop(first, last, body)

    def residue0(src):
        def body(y):
            g = [IN[c, y] for c in range(3)]
            v, n = around0(src, y)
            d = IN[3, y] + dot3(g, v)
            m = XM0[...] * ym0(y)
            for c in range(3):
                R0[c, y - 6] = m * (n[c] - 6.0 * v[c] - g[c] * d)

        loop(6, 16, body)

    def fold_rows(src, c, y, x, size):
        weights = (1.0, 3.0, 3.0, 1.0)
        total = None
        for kx in range(4):
            line = None
            for ky in range(4):
                term = src[c, y + ky, pl.ds(x + kx, size, stride=2)]
                term = term if weights[ky] == 1.0 else weights[ky] * term
                line = term if line is None else line + term
            line = line if weights[kx] == 1.0 else weights[kx] * line
            total = line if total is None else total + line
        return total

    def source1(cycle):
        def body(i):
            for c in range(3):
                C1[pl.ds(c * 32 + 8 * i, 8)] = fold_rows(R0, c, 2 * i, 7, 8)

        loop(0, 4, body)
        s = split_dot(C1[0:96], M01[...])
        for c in range(3):
            for j in range(2):
                at0 = 32 * c + 8 * j
                RS1[cycle, 2, 1, c, j] = jnp.where(low, s[at0:at0 + 8], s[at0 + 16:at0 + 24])

    low4 = iota((3, 2, 8, 128), 3) < 64
    low6 = iota((6, 2, 8, 128), 3) < 64

    def unpack(src, dst, mask, group):
        for dx in range(3):
            p = src[group, dx]
            other = pltpu.roll(p.reshape(-1, 128), 64, 1).reshape(p.shape)
            dst[:, pl.ds(4 * group, 2), 8 * dx:8 * dx + 8] = jnp.where(mask, p, 0.0)
            dst[:, pl.ds(4 * group + 2, 2), 8 * dx:8 * dx + 8] = jnp.where(mask, other, 0.0)

    def inverse1(y):
        m = damped_inverse([A1[f, y] for f in range(6)], W[1], XM1[...] * ym1(y))
        for f in range(6):
            I1[f, y] = m[f]

    def around1(src, y):
        centre, total = [], []
        for c in range(3):
            v = src[c, y]
            n = src[c, y - 1] + src[c, y + 1]
            n = n + (roll(v, 1, 0) + roll(v, -1, 0)) + (roll(v, 1, 1) + roll(v, -1, 1))
            centre.append(v)
            total.append(n)
        return centre, total

    def start1(y):
        new = sym([I1[f, y] for f in range(6)], [S1[c, y] for c in range(3)])
        for c in range(3):
            V1A[c, y] = new[c]

    def sweep1(src, dst, first, last):
        def body(y):
            v, n = around1(src, y)
            new = sym([I1[f, y] for f in range(6)], [S1[c, y] + W[1] * n[c] for c in range(3)])
            for c in range(3):
                dst[c, y] = KEEP * v[c] + new[c]

        loop(first, last, body)

    def residue1(src):
        def body(y):
            v, n = around1(src, y)
            av = sym([A1[f, y] for f in range(6)], v)
            m = XM1[...] * ym1(y)
            for c in range(3):
                R1[c, y - 7] = m * (S1[c, y] + W[1] * (n[c] - 6.0 * v[c]) - av[c])

        loop(7, 13, body)

    def source2(cycle):
        rows = []
        for c in range(3):
            for i in range(2):
                FS[0, 4 * (2 * c + i):4 * (2 * c + i) + 4] = fold_rows(R1, c, 2 * i, 7, 4)
        XG[cycle, 2, pl.ds(pl.multiple_of(gx * 8, 8), 8)] = pack(split_dot(FS[0, 0:24], M12[...]), 4)

    def shifts2(v):
        lane, r = iota(v.shape, 1), iota(v.shape, 0) & 7
        up = roll(v, -32, 1)
        xp = jnp.where(lane < 96, up, jnp.where(r == 7, 0.0, roll(up, -1, 0)))
        down = roll(v, 32, 1)
        xm = jnp.where(lane >= 32, down, jnp.where(r == 0, 0.0, roll(down, 1, 0)))
        return xm, xp

    def around2(src, first, last):
        centre, total = [], []
        for c in range(3):
            v3 = src[c, first:last]
            v = v3.reshape(-1, 128)
            z = iota(v.shape, 1) & 31
            xm, xp = shifts2(v)
            n = xm + xp + jnp.where(z == 0, 0.0, roll(v, 1, 1)) + jnp.where(z == 31, 0.0, roll(v, -1, 1))
            n = n.reshape(v3.shape) + (src[c, first - 1:last - 1] + src[c, first + 1:last + 1])
            centre.append(v3)
            total.append(n)
        return centre, total

    def start2(cycle, first, last):
        new = sym([I2[f, first:last] for f in range(6)], [S2[cycle, c, first:last] for c in range(3)])
        for c in range(3):
            V2A[c, first:last] = new[c]

    def sweep2(cycle, src, dst, first, last):
        v, n = around2(src, first, last)
        p = [S2[cycle, c, first:last] + W[2] * n[c] for c in range(3)]
        new = sym([I2[f, first:last] for f in range(6)], p)
        for c in range(3):
            dst[c, first:last] = KEEP * v[c] + new[c]

    def source3(cycle):
        v, n = around2(V2B, 7, 11)
        av = sym([A2[f, 7:11] for f in range(6)], v)
        rows = []
        for c in range(3):
            r = YM2[7:11] * (S2[cycle, c, 7:11] + W[2] * (n[c] - 6.0 * v[c]) - av[c])
            f = r[0] + 3.0 * (r[1] + r[2]) + r[3]
            xm, xp = shifts2(f)
            _, more = shifts2(3.0 * f + xp)
            rows.append(xm + 3.0 * f + more)
        SG[cycle, 96:104] = pack(split_dot(jnp.concatenate(rows, axis=0), M23[...]), 4)

    lane3 = iota((24, 128), 1)

    def shifts3(a, b):
        ua, ub = roll(a, -16, 1), roll(b, -16, 1)
        da, db = roll(a, 16, 1), roll(b, 16, 1)
        up = jnp.where(lane3 < 112, ua, ub), jnp.where(lane3 < 112, ub, 0.0)
        down = jnp.where(lane3 >= 16, da, 0.0), jnp.where(lane3 >= 16, db, da)
        return down, up

    def solve3(cycle):
        s = [[SG[cycle, pl.ds(2 * c + h, 24, stride=8)] for h in range(2)] for c in range(3)]
        for h in range(2):
            new = sym([I3[f, h] for f in range(6)], [s[c][h] for c in range(3)])
            for c in range(3):
                V3[c, h] = new[c]

        def body(i):
            v = [[V3[c, h] for h in range(2)] for c in range(3)]
            p = [[None, None] for c in range(3)]
            for c in range(3):
                down, up = shifts3(v[c][0], v[c][1])
                for h in range(2):
                    a = v[c][h]
                    n = roll(a, 1, 0) + roll(a, -1, 0) + down[h] + up[h]
                    n = n + jnp.where((lane3 & 15) == 0, 0.0, roll(a, 1, 1))
                    n = n + jnp.where((lane3 & 15) == 15, 0.0, roll(a, -1, 1))
                    p[c][h] = SG[cycle, pl.ds(2 * c + h, 24, stride=8)] + W[3] * n
            for h in range(2):
                new = sym([I3[f, h] for f in range(6)], [p[c][h] for c in range(3)])
                for c in range(3):
                    V3[c, h] = KEEP * v[c][h] + new[c]

        loop(0, 7, body)

    def spread3():
        for c in range(3):
            a, b = V3[c, 0], V3[c, 1]
            down, up = shifts3(a, b)
            for h, v in enumerate((a, b)):
                even = 0.75 * v + 0.25 * down[h]
                odd = 0.75 * v + 0.25 * up[h]
                E3[0, pl.ds(32 * c + h, 16, stride=2)] = even[8:24]
                E3[1, pl.ds(32 * c + h, 16, stride=2)] = odd[8:24]
        fine = split_dot(E3[0], M32[0]) + split_dot(E3[1], M32[1])
        for q in range(4):
            P3[pl.ds(q, 96, stride=4)] = fine[:, 128 * q:128 * q + 128]
        for c in range(3):
            def planes(i):
                return P3[128 * c + 8 * i:128 * c + 8 * i + 56].reshape(7, 8, 128)

            before, mid, after = planes(0), planes(1), planes(2)
            even = 0.75 * mid + 0.25 * before
            odd = 0.75 * mid + 0.25 * after
            for i in range(7):
                y = 2 + 2 * i
                V2B[c, y] = (V2B[c, y] + even[i]) * YM2[y]
                V2B[c, y + 1] = (V2B[c, y + 1] + odd[i]) * YM2[y + 1]

    def spread2():
        for c in range(3):
            v = V2B[c, 4:14].reshape(80, 128)
            xm, xp = shifts2(v)
            E21[0, 8 + 80 * c:88 + 80 * c] = 0.75 * v + 0.25 * xm
            E21[1, 8 + 80 * c:88 + 80 * c] = 0.75 * v + 0.25 * xp
        lines = []
        for j in range(3):
            inside = jnp.where((gx + j >= 1) & (gx + j <= 8), 1.0, 0.0).astype(F32)
            for eo in range(2):
                lines.append(E21[eo, pl.ds(7 + gx + j, 32, stride=8)] * inside)
        fine = split_dot(jnp.concatenate(lines, axis=0), M21[...])
        for j in range(3):
            for eo in range(2):
                for q in range(4):
                    at0 = 32 * (2 * j + eo)
                    P21[pl.ds(8 * j + 2 * q + eo, 32, stride=24)] = fine[at0:at0 + 32, 128 * q:128 * q + 128]

    def add2(first, last):
        def body(p):
            for c in range(3):
                def lines_of(i):
                    return P21[pl.ds(pl.multiple_of((10 * c + i) * 24, 8), 24)]

                mid = 0.75 * lines_of(p)
                even = mid + 0.25 * lines_of(p - 1)
                odd = mid + 0.25 * lines_of(p + 1)
                V1B[c, 2 * p] = (V1B[c, 2 * p] + even) * (XM1[...] * ym1(2 * p))
                V1B[c, 2 * p + 1] = (V1B[c, 2 * p + 1] + odd) * (XM1[...] * ym1(2 * p + 1))

        loop(first, last, body)

    def spread1(first, last):
        for c in range(3):
            CZ[c] = split_dot(V1B[c, 4:16].reshape(288, 128), M10[...]).reshape(12, 24, 128)

        def body(p):
            for b in range(2):
                y = 2 * p - 1 + b
                m = XM0[...] * ym0(y)
                for c in range(3):
                    a = 0.75 * CZ[c, p] + 0.25 * CZ[c, p - 1 + 2 * b]
                    mid = 0.75 * roll(a, -4, 0)
                    TMP[b, c, pl.ds(0, 16, stride=2)] = (mid + 0.25 * roll(a, -3, 0))[0:16]
                    TMP[b, c, pl.ds(1, 16, stride=2)] = (mid + 0.25 * roll(a, -5, 0))[0:16]
                    VB[c, y] = (VB[c, y] + TMP[b, c]) * m

        loop(first, last, body)

    for cycle in range(2):
        if cycle == 0:
            far_in = [input_copy((dy, 0), y_far[dy], (0, 8, 16)) for dy in (1, -1)]
            loop(4, 18, start0)
            sweep0(VA, VB, 5, 17)
        else:
            sweep0(VB, VA, 4, 18)
            sweep0(VA, VB, 5, 17)
        residue0(VB)
        source1(cycle)
        s1 = RS1.at[cycle]
        s1_near = [box_copy(s1, s1, peer) for peer in NEAR]
        sent += s1_near

        if cycle == 0:
            received(a2_x)
            rows = []
            for f in range(6):
                one = XA[pl.ds(2 * f, 8, stride=16)]
                two = XA[pl.ds(2 * f + 1, 8, stride=16)]
                A2[f, 8] = one
                A2[f, 9] = two
                rows.append(one + two)
            RA3[192:208] = pack(split_dot(jnp.concatenate(rows, axis=0), P23[...]), 4)
            a2_y = [
                send(A2.at[:, 8:10], A2.at[:, pl.ds(8 - 2 * d * side, 2)], (d * side, 0)) for d in (3, 2, 1)
            ]
            a2_y.append(
                send(A2.at[:, pl.ds(9 - core, 1)], A2.at[:, pl.ds(9 - core - 8 * side, 1)], (4 * side, 0))
            )
            a3_y = [
                send(RA3.at[192:208], RA3.at[pl.ds(pl.multiple_of(16 * (12 - d * side), 16), 16)], (d * side, 0))
                for d in range(1, 12)
            ]
            sent += a2_y + a3_y
            received(a1_near)
            loop(1, 4, functools.partial(unpack, RA1, A1, low6))
            loop(4, 16, inverse1)

        received(s1_near)
        loop(1, 4, functools.partial(unpack, s1, S1, low4))
        loop(5, 15, start1)
        sweep1(V1A, V1B, 6, 14)
        residue1(V1B)
        source2(cycle)
        own = pl.ds(pl.multiple_of(gx * 8, 8), 8)
        s2 = {
            (dy, dx): send(XG.at[cycle, 2, own], XG.at[cycle, 2 - dy, own], (dy, dx)) for dy, dx in SHEET
        }
        sent += s2.values()
        if cycle == 0:
            s1_far = [box_copy(s1, s1, peer) for peer in OUTER]
        else:
            s1_far = [
                send(s1.at[2, 1, :, row:row + 1], s1.at[2 - dy, 1 - dx, :, row:row + 1], (dy, dx))
                for dy, dx in OUTER
                for row in [1 if dy > 0 else 0]
            ]
        sent += s1_far
        if cycle == 0:
            a1_far = [box_copy(RA1, RA1, peer) for peer in OUTER]
            sent += a1_far
            received(a2_y)
            a2_swap = pl.ds(1 + 9 * core, 7)
            a2_y = [send(A2.at[:, a2_swap], A2.at[:, a2_swap], twin)]
            received(a3_y)
            a3_swap = pl.ds(pl.multiple_of(16 + 192 * core, 16), 176)
            a3_y = [send(RA3.at[a3_swap], RA3.at[a3_swap], twin)]
            sent += a2_y + a3_y
            received(a2_y)
            m = damped_inverse([A2[f] for f in range(6)], W[2], YM2[...])
            for f in range(6):
                I2[f] = m[f]
        received(s2.values())
        for i in range(5):
            for c in range(3):
                for j in range(2):
                    S2[cycle, c, 4 + 2 * i + j] = XG[cycle, i, pl.ds(2 * c + j, 8, stride=8)]
        start2(cycle, 5, 13)
        sweep2(cycle, V2A, V2B, 6, 12)
        source3(cycle)
        reach = [d for d in RING if abs(d) <= 11 - cycle]
        s3 = [send(SG.at[cycle, 96:104], SG.at[cycle, 96 - 8 * d:104 - 8 * d], (d, 0)) for d in reach]

        s2_far = [
            send(S2.at[cycle, :, 8:10], S2.at[cycle, :, pl.ds(8 - 6 * side, 2)], (3 * side, 0))
        ]
        if cycle == 0:
            s2_far.append(
                send(
                    S2.at[cycle, :, pl.ds(9 - core, 1)],
                    S2.at[cycle, :, pl.ds(9 - core - 8 * side, 1)],
                    (4 * side, 0),
                )
            )
            for dy in (1, -1):
                for dx in (1, -1):
                    far_in.append(input_copy((dy, dx), y_far[dy], x_wide[dx]))
                    far_in.append(input_copy((dy, dx), y_near[dy], x_rest[dx]))
            sent += far_in
            received(a3_y)
            place = iota((24, 128), 0) + (gy - 12)
            mask = jnp.where((place >= 0) & (place < 32), 1.0, 0.0)
            for h in range(2):
                m = damped_inverse([RA3[pl.ds(2 * f + h, 24, stride=16)] for f in range(6)], W[3], mask)
                for f in range(6):
                    I3[f, h] = m[f]
        received(s1_far)
        for group in (0, 4):
            unpack(s1, S1, low4, group)
        received(s2_far)
        swap = pl.ds(1 + 13 * core, 3) if cycle == 0 else pl.ds(2 + 12 * core, 2)
        s2_swap = [send(S2.at[cycle, :, swap], S2.at[cycle, :, swap], twin)]
        if cycle == 1:
            loop(3, 5, start1)
            loop(15, 17, start1)
            sweep1(V1A, V1B, 4, 6)
            sweep1(V1A, V1B, 14, 16)
            for copy in sent:
                copy.wait_send()
        received(s2_swap)
        start2(cycle, 1, 5)
        start2(cycle, 13, 17)
        sweep2(cycle, V2A, V2B, 2, 6)
        sweep2(cycle, V2A, V2B, 12, 16)
        late = s3 + s2_far + s2_swap
        if cycle == 0:
            sent += late

        received(s3)
        solve3(cycle)
        spread3()
        sweep2(cycle, V2B, V2A, 3, 15)
        sweep2(cycle, V2A, V2B, 4, 14)
        spread2()
        if cycle == 0:
            received(a1_far)
            for group in (0, 4):
                unpack(RA1, A1, low6, group)
            loop(0, 4, inverse1)
            loop(16, 20, inverse1)
            loop(1, 5, start1)
            loop(15, 19, start1)
            sweep1(V1A, V1B, 2, 6)
            sweep1(V1A, V1B, 14, 18)
            add2(1, 9)
            sweep1(V1B, V1A, 3, 17)
            sweep1(V1A, V1B, 4, 16)
            received(far_in)
            loop(0, 7, start0)
            loop(15, 22, start0)
            sweep0(VA, VB, 1, 8)
            sweep0(VA, VB, 14, 21)
            spread1(1, 11)
            sweep0(VB, VA, 2, 20)
            sweep0(VA, VB, 3, 19)
        else:
            add2(2, 8)
            sweep1(V1B, V1A, 5, 15)
            sweep1(V1A, V1B, 6, 14)
            spread1(3, 9)
            sweep0(VB, VA, 6, 16)

            def last(y):
                new = swept0(VA, y)
                for c in range(3):
                    out[c, y - 7] = new[c][8:24]

            loop(7, 15, last)
            for copy in late:
                copy.wait_send()


TRANSFERS = 220


def local(spatial_grad, temporal_grad):
    def v(*shape, dtype=F32):
        return pltpu.VMEM(shape, dtype)

    def m(*shape):
        return pltpu.VMEM(shape, BF16)

    scratch = [
        v(4, 22, 32, 128), v(22, 32, 128), v(3, 22, 32, 128), v(3, 22, 32, 128), v(3, 10, 32, 128),
        v(32, 128), v(6, 32, 128), v(3, 12, 24, 128), v(2, 3, 32, 128),
        v(5, 3, 6, 2, 8, 128), v(6, 20, 24, 128), v(6, 20, 24, 128), v(2, 5, 3, 3, 2, 8, 128), v(3, 20, 24, 128),
        v(3, 20, 24, 128), v(3, 20, 24, 128), v(3, 6, 24, 128), v(24, 128),
        v(192, 128), v(192, 128), v(128, 128), v(128, 128), v(6, 18, 8, 128), v(6, 18, 8, 128), v(2, 5, 64, 128),
        v(2, 3, 18, 8, 128), v(3, 18, 8, 128), v(3, 18, 8, 128), v(18, 8, 128), v(2, 272, 128), v(768, 128),
        v(384, 128), v(6, 2, 24, 128), v(2, 192, 128), v(3, 2, 24, 128), v(2, 96, 128), v(384, 128),
        m(128, 128), m(128, 128), m(128, 128), m(128, 128), m(128, 128), m(128, 128),
        m(2, 128, 512), m(128, 512), m(128, 128),
        pltpu.SemaphoreType.DMA((2,)),
        pltpu.SemaphoreType.DMA((TRANSFERS,)),
        pltpu.SemaphoreType.DMA((TRANSFERS,)),
    ]
    return pl.pallas_call(
        kernel,
        out_shape=jax.ShapeDtypeStruct(spatial_grad.shape, F32),
        in_specs=[pl.BlockSpec(memory_space=pl.ANY)] * 2,
        out_specs=pl.BlockSpec(memory_space=pltpu.VMEM),
        scratch_shapes=scratch,
        compiler_params=pltpu.CompilerParams(
            collective_id=0, has_side_effects=True, vmem_limit_bytes=60 * 2**20
        ),
        name="flow",
    )(spatial_grad, temporal_grad)


def solution(mesh):
    placed = (P(None, "gy", "gx", None), P("gy", "gx", None))
    return jax.shard_map(
        local, mesh=mesh, in_specs=placed, out_specs=P(None, "gy", "gx", None), check_vma=False
    )
```

```python
import functools

import jax
import jax.numpy as jnp
from jax import lax
from jax.experimental import pallas as pl
from jax.experimental.pallas import tpu as pltpu
from jax.sharding import PartitionSpec as P

MESH = pl.DeviceIdType.MESH
F32 = jnp.float32
BF16 = jnp.bfloat16
GROUP = 2
UNROLL = 8
KEEP = 0.2
DAMP = 0.8
W = (1.0, 0.25, 0.0625, 0.015625)

NEAR = [(a, b) for a in (-1, 0, 1) for b in (-1, 0, 1) if (a, b) != (0, 0)]
OUTER = [(a, b) for a in (-2, 2) for b in (-1, 0, 1)]
BOX = NEAR + OUTER
SHEET = [(a, b) for a in (2, -2, 1, -1, 0) for b in range(8) if (a, b) != (0, 0)]
RING = [s * d for d in range(1, 12) for s in (1, -1)]


def loop(first, last, body):
    def step(i, carry):
        body(i)
        return carry

    lax.fori_loop(first, last, step, 0, unroll=min(UNROLL, last - first))


def planes(first, last, compute, store):
    def body(i):
        y = first + GROUP * i
        new = [compute(y + k) for k in range(GROUP)]
        for k in range(GROUP):
            store(y + k, new[k])

    assert (last - first) % GROUP == 0
    loop(0, (last - first) // GROUP, body)


def iota(shape, dim):
    return lax.broadcasted_iota(jnp.int32, shape, dim)


def roll(x, shift, axis):
    return pltpu.roll(x, shift % x.shape[axis], axis)


def split_dot(x, matrix):
    high = x.astype(BF16).astype(F32)
    both = jnp.concatenate([high, x - high], axis=0).astype(BF16)
    out = jnp.dot(both, matrix, preferred_element_type=F32)
    rows = x.shape[0]
    return out[:rows] + out[rows:]


def fold_weight(d):
    return jnp.where((d == 0) | (d == 1), 3.0, jnp.where((d == -1) | (d == 2), 1.0, 0.0))


def spread_weight(d):
    return jnp.where((d == 0) | (d == 1), 0.75, jnp.where((d == -1) | (d == 2), 0.25, 0.0))


def sym(m, v):
    return [
        m[0] * v[0] + m[3] * v[1] + m[4] * v[2],
        m[3] * v[0] + m[1] * v[1] + m[5] * v[2],
        m[4] * v[0] + m[5] * v[1] + m[2] * v[2],
    ]


def damped_inverse(m, weight, mask):
    dx, dy, dz = (m[k] + 6.0 * weight for k in range(3))
    xy, xz, yz = m[3], m[4], m[5]
    cof = [
        dy * dz - yz * yz,
        dx * dz - xz * xz,
        dx * dy - xy * xy,
        xz * yz - xy * dz,
        xy * yz - dy * xz,
        xy * xz - dx * yz,
    ]
    det = dx * cof[0] + xy * cof[3] + xz * cof[4]
    scale = mask * DAMP / det
    return [c * scale for c in cof]


def kernel(
    sg, tg, out,
    IN, Q, VA, VB, R0, XM0, FS, CZ, TMP,
    RA1, A1, I1, RS1, S1, V1A, V1B, R1, XM1,
    C1, C2, F, XA, A2, I2, XG, S2, V2A, V2B, YM2, E21, P21,
    RA3, I3, SG, V3, E3, P3,
    M01, M12, M23, P01, P12, P23, M32, M21, M10,
    lsem, ssem, rsem,
):
    gy = lax.axis_index("gy")
    gx = lax.axis_index("gx")

    core = lax.rem(gx, 2)
    side = 1 - 2 * core
    twin = (0, side)

    def at(dy, dx):
        return lax.rem(gy + dy + 32, 32), lax.rem(gx + dx + 8, 8)

    S2[...] = jnp.zeros_like(S2)
    A2[...] = jnp.zeros_like(A2)
    SG[...] = jnp.zeros_like(SG)
    RA3[...] = jnp.zeros_like(RA3)
    barrier = pltpu.get_barrier_semaphore()
    everyone = SHEET + [(d, 0) for d in RING if abs(d) > 2]
    for peer in everyone:
        pl.semaphore_signal(barrier, inc=1, device_id=at(*peer), device_id_type=MESH)

    load_g = pltpu.make_async_copy(sg, IN.at[0:3, 7:15, 8:24], lsem.at[0])
    load_t = pltpu.make_async_copy(tg, IN.at[3, 7:15, 8:24], lsem.at[1])
    load_g.start()
    load_t.start()

    count = [0]

    def send(src, dst, peer):
        k = count[0]
        count[0] += 1
        copy = pltpu.make_async_remote_copy(
            src_ref=src, dst_ref=dst, send_sem=ssem.at[k], recv_sem=rsem.at[k],
            device_id=at(*peer), device_id_type=MESH,
        )
        copy.start()
        return copy

    def received(copies):
        for copy in copies:
            copy.wait_recv()

    sent = []

    load_g.wait()
    load_t.wait()
    pl.semaphore_wait(barrier, len(everyone))

    def input_copy(peer, rows, columns):
        (y0, y1, height), (x0, x1, width) = rows, columns
        return send(
            IN.at[:, 7 + y0:7 + y0 + height, 8 + x0:8 + x0 + width],
            IN.at[:, y1:y1 + height, x1:x1 + width],
            peer,
        )

    y_near = {1: (5, 4, 3), -1: (0, 15, 3)}
    y_far = {1: (1, 0, 4), -1: (3, 18, 4)}
    x_near = {1: (13, 5, 3), -1: (0, 24, 3)}
    x_some = {1: (12, 4, 4), -1: (0, 24, 4)}
    x_rest = {1: (9, 1, 4), -1: (3, 27, 4)}
    x_all = {1: (8, 0, 8), -1: (0, 24, 8)}

    near_in = [input_copy((dy, dx), y_near[dy], x_near[dx]) for dy in (1, -1) for dx in (1, -1)]
    near_in += [input_copy((dy, 0), y_near[dy], (0, 8, 16)) for dy in (1, -1)]
    near_in += [input_copy((0, dx), (0, 7, 8), x_all[dx]) for dx in (1, -1)]
    def lanes(shape):
        return iota(shape, 0), iota(shape, 1)

    k, n = lanes((128, 128))
    M01[...] = (fold_weight(k - 2 * (n & 63)) * (1.0 / 512.0)).astype(BF16)
    P01[...] = jnp.where((k >> 1) == (n & 63), 0.125, 0.0).astype(BF16)
    M12[...] = jnp.where(k < 64, fold_weight(k - 2 * (n & 31)) * (1.0 / 512.0), 0.0).astype(BF16)
    P12[...] = jnp.where((k < 64) & ((k >> 1) == (n & 31)), 0.125, 0.0).astype(BF16)
    part = (n & 31) >> 4
    M23[...] = jnp.where(
        (k >> 5) == 2 * part, fold_weight((k & 31) - 2 * (n & 15)) * (1.0 / 512.0), 0.0
    ).astype(BF16)
    P23[...] = jnp.where(((k >> 6) == part) & (((k & 31) >> 1) == (n & 15)), 0.125, 0.0).astype(BF16)
    M10[...] = jnp.where(k < 64, spread_weight(n - 2 * k), 0.0).astype(BF16)
    for q in range(4):
        M21[:, 128 * q:128 * q + 128] = jnp.where(
            ((k >> 5) == q) & (n < 64), spread_weight(n - 2 * (k & 31)), 0.0
        ).astype(BF16)
        for eo in range(2):
            xs = n >> 5
            fits = ((xs & 1) == eo) & ((k >> 4) == 2 * q + (xs >> 1))
            M32[eo, :, 128 * q:128 * q + 128] = jnp.where(
                fits, spread_weight((n & 31) - 2 * (k & 15)), 0.0
            ).astype(BF16)

    row = iota((32, 128), 0) + (16 * gx - 8)
    XM0[...] = jnp.where((row >= 0) & (row < 128), 1.0, 0.0)
    row = iota((24, 128), 0) + (8 * gx - 8)
    XM1[...] = jnp.where((row >= 0) & (row < 64) & (iota((24, 128), 1) < 64), 1.0, 0.0)
    plane = iota((18, 8, 128), 0) + (2 * gy - 8)
    YM2[...] = jnp.where((plane >= 0) & (plane < 64), 1.0, 0.0)
    E21[...] = jnp.zeros_like(E21)

    def ym(first, length, y):
        place = first + y
        return jnp.where((place >= 0) & (place < length), 1.0, 0.0).astype(F32)

    def ym0(y):
        return ym(8 * gy - 7, 256, y)

    def ym1(y):
        return ym(4 * gy - 8, 128, y)

    def pack(rows, group):
        size = rows.shape[0]
        keep = (iota(rows.shape, 1) >> 5) == (iota(rows.shape, 0) & 3)
        F[0:size] = jnp.where(keep, rows, 0.0)
        kept = 8 * ((size // group + 7) // 8)
        total = F[pl.ds(0, kept, stride=group)]
        for r in range(1, group):
            total = total + F[pl.ds(r, kept, stride=group)]
        return total

    F[...] = jnp.zeros_like(F)

    def own_coeffs(i):
        def products(y):
            g = [IN[c, y, 8:24] for c in range(3)]
            return [g[0] * g[0], g[1] * g[1], g[2] * g[2], g[0] * g[1], g[0] * g[2], g[1] * g[2]]

        one, two = products(7 + 2 * i), products(8 + 2 * i)
        for f in range(6):
            FS[f, 0:16] = one[f] + two[f]
        for f in range(6):
            C1[pl.ds(f * 32 + 8 * i, 8)] = FS[f, pl.ds(0, 8, stride=2)] + FS[f, pl.ds(1, 8, stride=2)]

    loop(0, 4, own_coeffs)
    C2[...] = split_dot(C1[...], P01[...])
    low = iota((8, 128), 1) < 64
    for f in range(6):
        for j in range(2):
            RA1[2, 1, f, j] = jnp.where(
                low, C2[32 * f + 8 * j:32 * f + 8 * j + 8], C2[32 * f + 8 * j + 16:32 * f + 8 * j + 24]
            )
    halved = C2[pl.ds(0, 96, stride=2)] + C2[pl.ds(1, 96, stride=2)]
    XA[pl.ds(pl.multiple_of(gx * 16, 16), 16)] = pack(split_dot(halved, P12[...]), 8)

    own_a2 = pl.ds(pl.multiple_of(gx * 16, 16), 16)
    a2_x = [send(XA.at[own_a2], XA.at[own_a2], (0, d)) for d in range(1, 8)]

    def box_copy(src, dst, peer):
        return send(src.at[2, 1], dst.at[2 - peer[0], 1 - peer[1]], peer)

    def outer_copy(buf, peer, cycle):
        dy, dx = peer
        rows = slice(0, 2) if cycle == 0 else (slice(1, 2) if dy > 0 else slice(0, 1))
        wide = 3 if cycle == 0 else 1
        columns = {1: slice(8 - wide, 8), 0: slice(0, 8), -1: slice(0, wide)}[dx]
        return send(buf.at[2, 1, :, rows, columns], buf.at[2 - dy, 1 - dx, :, rows, columns], peer)

    a1_near = [box_copy(RA1, RA1, peer) for peer in NEAR]
    sent += near_in + a2_x + a1_near
    received(near_in)

    lane0 = iota((32, 128), 1)
    first_lane, last_lane = lane0 == 0, lane0 == 127

    def around0(src, y):
        centre, total = [], []
        for c in range(3):
            v = src[c, y]
            n = src[c, y - 1] + src[c, y + 1]
            n = n + (roll(v, 1, 0) + roll(v, -1, 0))
            n = n + jnp.where(first_lane, 0.0, roll(v, 1, 1)) + jnp.where(last_lane, 0.0, roll(v, -1, 1))
            centre.append(v)
            total.append(n)
        return centre, total

    def dot3(a, b):
        return a[0] * b[0] + a[1] * b[1] + a[2] * b[2]

    def start0(y):
        g = [IN[c, y] for c in range(3)]
        q = XM0[...] * ym0(y) * (DAMP / 6.0) / (6.0 + dot3(g, g))
        scale = -6.0 * IN[3, y] * q
        return q, [scale * g[c] for c in range(3)]

    def store0(y, new):
        Q[y] = new[0]
        for c in range(3):
            VA[c, y] = new[1][c]

    def swept0(src, y):
        g = [IN[c, y] for c in range(3)]
        t = IN[3, y]
        v, n = around0(src, y)
        p = [n[c] - t * g[c] for c in range(3)]
        d = dot3(g, p) * Q[y]
        scale = XM0[...] * (ym0(y) * (DAMP / 6.0))
        return [KEEP * v[c] + scale * p[c] - d * g[c] for c in range(3)]

    def sweep0(src, dst, first, last):
        def store(y, new):
            for c in range(3):
                dst[c, y] = new[c]

        planes(first, last, functools.partial(swept0, src), store)

    def residue0(src):
        def compute(y):
            g = [IN[c, y] for c in range(3)]
            v, n = around0(src, y)
            d = IN[3, y] + dot3(g, v)
            m = XM0[...] * ym0(y)
            return [m * (n[c] - 6.0 * v[c] - g[c] * d) for c in range(3)]

        def store(y, new):
            for c in range(3):
                R0[c, y - 6] = new[c]

        planes(6, 16, compute, store)

    def fold_rows(src, c, y, x, size):
        weights = (1.0, 3.0, 3.0, 1.0)
        total = None
        for kx in range(4):
            line = None
            for ky in range(4):
                term = src[c, y + ky, pl.ds(x + kx, size, stride=2)]
                term = term if weights[ky] == 1.0 else weights[ky] * term
                line = term if line is None else line + term
            line = line if weights[kx] == 1.0 else weights[kx] * line
            total = line if total is None else total + line
        return total

    def source1(cycle):
        lines = [fold_rows(R0, c, 2 * i, 7, 8) for c in range(3) for i in range(4)]
        s = split_dot(jnp.concatenate(lines, axis=0), M01[...])
        for c in range(3):
            for j in range(2):
                at0 = 32 * c + 8 * j
                RS1[cycle, 2, 1, c, j] = jnp.where(low, s[at0:at0 + 8], s[at0 + 16:at0 + 24])

    low4 = iota((3, 2, 8, 128), 3) < 64
    low6 = iota((6, 2, 8, 128), 3) < 64

    def unpack(src, dst, mask, group):
        for dx in range(3):
            p = src[group, dx]
            other = pltpu.roll(p.reshape(-1, 128), 64, 1).reshape(p.shape)
            dst[:, pl.ds(4 * group, 2), 8 * dx:8 * dx + 8] = jnp.where(mask, p, 0.0)
            dst[:, pl.ds(4 * group + 2, 2), 8 * dx:8 * dx + 8] = jnp.where(mask, other, 0.0)

    def inverse1(y):
        m = damped_inverse([A1[f, y] for f in range(6)], W[1], XM1[...] * ym1(y))
        for f in range(6):
            I1[f, y] = m[f]

    def around1(src, y):
        centre, total = [], []
        for c in range(3):
            v = src[c, y]
            n = src[c, y - 1] + src[c, y + 1]
            n = n + (roll(v, 1, 0) + roll(v, -1, 0)) + (roll(v, 1, 1) + roll(v, -1, 1))
            centre.append(v)
            total.append(n)
        return centre, total

    def start1(y):
        new = sym([I1[f, y] for f in range(6)], [S1[c, y] for c in range(3)])
        for c in range(3):
            V1A[c, y] = new[c]

    def sweep1(src, dst, first, last):
        def compute(y):
            v, n = around1(src, y)
            new = sym([I1[f, y] for f in range(6)], [S1[c, y] + W[1] * n[c] for c in range(3)])
            return [KEEP * v[c] + new[c] for c in range(3)]

        def store(y, new):
            for c in range(3):
                dst[c, y] = new[c]

        planes(first, last, compute, store)

    def residue1(src):
        def compute(y):
            v, n = around1(src, y)
            av = sym([A1[f, y] for f in range(6)], v)
            m = XM1[...] * ym1(y)
            return [m * (S1[c, y] + W[1] * (n[c] - 6.0 * v[c]) - av[c]) for c in range(3)]

        def store(y, new):
            for c in range(3):
                R1[c, y - 7] = new[c]

        planes(7, 13, compute, store)

    def source2(cycle):
        lines = [fold_rows(R1, c, 2 * i, 7, 4) for i in range(2) for c in range(3)]
        for k in range(6):
            FS[0, 4 * k:4 * k + 4] = lines[k]
        XG[cycle, 2, pl.ds(pl.multiple_of(gx * 8, 8), 8)] = pack(split_dot(FS[0, 0:24], M12[...]), 4)

    def shifts2(v):
        lane, r = iota(v.shape, 1), iota(v.shape, 0) & 7
        up = roll(v, -32, 1)
        xp = jnp.where(lane < 96, up, jnp.where(r == 7, 0.0, roll(up, -1, 0)))
        down = roll(v, 32, 1)
        xm = jnp.where(lane >= 32, down, jnp.where(r == 0, 0.0, roll(down, 1, 0)))
        return xm, xp

    def around2(src, first, last):
        centre, total = [], []
        for c in range(3):
            v3 = src[c, first:last]
            v = v3.reshape(-1, 128)
            z = iota(v.shape, 1) & 31
            xm, xp = shifts2(v)
            n = xm + xp + jnp.where(z == 0, 0.0, roll(v, 1, 1)) + jnp.where(z == 31, 0.0, roll(v, -1, 1))
            n = n.reshape(v3.shape) + (src[c, first - 1:last - 1] + src[c, first + 1:last + 1])
            centre.append(v3)
            total.append(n)
        return centre, total

    def start2(cycle, first, last):
        new = sym([I2[f, first:last] for f in range(6)], [S2[cycle, c, first:last] for c in range(3)])
        for c in range(3):
            V2A[c, first:last] = new[c]

    def sweep2(cycle, src, dst, first, last):
        v, n = around2(src, first, last)
        p = [S2[cycle, c, first:last] + W[2] * n[c] for c in range(3)]
        new = sym([I2[f, first:last] for f in range(6)], p)
        for c in range(3):
            dst[c, first:last] = KEEP * v[c] + new[c]

    def source3(cycle):
        v, n = around2(V2B, 7, 11)
        av = sym([A2[f, 7:11] for f in range(6)], v)
        rows = []
        for c in range(3):
            r = YM2[7:11] * (S2[cycle, c, 7:11] + W[2] * (n[c] - 6.0 * v[c]) - av[c])
            f = r[0] + 3.0 * (r[1] + r[2]) + r[3]
            xm, xp = shifts2(f)
            _, more = shifts2(3.0 * f + xp)
            rows.append(xm + 3.0 * f + more)
        SG[cycle, 96:104] = pack(split_dot(jnp.concatenate(rows, axis=0), M23[...]), 4)

    lane3 = iota((24, 128), 1)

    def shifts3(a, b):
        ua, ub = roll(a, -16, 1), roll(b, -16, 1)
        da, db = roll(a, 16, 1), roll(b, 16, 1)
        up = jnp.where(lane3 < 112, ua, ub), jnp.where(lane3 < 112, ub, 0.0)
        down = jnp.where(lane3 >= 16, da, 0.0), jnp.where(lane3 >= 16, db, da)
        return down, up

    def solve3(cycle):
        s = [[SG[cycle, pl.ds(2 * c + h, 24, stride=8)] for h in range(2)] for c in range(3)]
        for h in range(2):
            new = sym([I3[f, h] for f in range(6)], [s[c][h] for c in range(3)])
            for c in range(3):
                V3[c, h] = new[c]

        def body(i):
            v = [[V3[c, h] for h in range(2)] for c in range(3)]
            p = [[None, None] for c in range(3)]
            for c in range(3):
                down, up = shifts3(v[c][0], v[c][1])
                for h in range(2):
                    a = v[c][h]
                    n = roll(a, 1, 0) + roll(a, -1, 0) + down[h] + up[h]
                    n = n + jnp.where((lane3 & 15) == 0, 0.0, roll(a, 1, 1))
                    n = n + jnp.where((lane3 & 15) == 15, 0.0, roll(a, -1, 1))
                    p[c][h] = SG[cycle, pl.ds(2 * c + h, 24, stride=8)] + W[3] * n
            for h in range(2):
                new = sym([I3[f, h] for f in range(6)], [p[c][h] for c in range(3)])
                for c in range(3):
                    V3[c, h] = KEEP * v[c][h] + new[c]

        loop(0, 7, body)

    def spread3():
        for c in range(3):
            a, b = V3[c, 0], V3[c, 1]
            down, up = shifts3(a, b)
            for h, v in enumerate((a, b)):
                even = 0.75 * v + 0.25 * down[h]
                odd = 0.75 * v + 0.25 * up[h]
                E3[0, pl.ds(32 * c + h, 16, stride=2)] = even[8:24]
                E3[1, pl.ds(32 * c + h, 16, stride=2)] = odd[8:24]
        fine = split_dot(E3[0], M32[0]) + split_dot(E3[1], M32[1])
        for q in range(4):
            P3[pl.ds(q, 96, stride=4)] = fine[:, 128 * q:128 * q + 128]
        for c in range(3):
            def planes(i):
                return P3[128 * c + 8 * i:128 * c + 8 * i + 56].reshape(7, 8, 128)

            before, mid, after = planes(0), planes(1), planes(2)
            even = 0.75 * mid + 0.25 * before
            odd = 0.75 * mid + 0.25 * after
            for i in range(7):
                y = 2 + 2 * i
                V2B[c, y] = (V2B[c, y] + even[i]) * YM2[y]
                V2B[c, y + 1] = (V2B[c, y + 1] + odd[i]) * YM2[y + 1]

    def spread2():
        for c in range(3):
            v = V2B[c, 4:14].reshape(80, 128)
            xm, xp = shifts2(v)
            E21[0, 8 + 80 * c:88 + 80 * c] = 0.75 * v + 0.25 * xm
            E21[1, 8 + 80 * c:88 + 80 * c] = 0.75 * v + 0.25 * xp
        lines = []
        for j in range(3):
            inside = (gx + j >= 1) & (gx + j <= 8)
            for eo in range(2):
                lines.append(jnp.where(inside, E21[eo, pl.ds(7 + gx + j, 32, stride=8)], 0.0))
        fine = split_dot(jnp.concatenate(lines, axis=0), M21[...])
        for j in range(3):
            for eo in range(2):
                for q in range(4):
                    at0 = 32 * (2 * j + eo)
                    P21[pl.ds(8 * j + 2 * q + eo, 32, stride=24)] = fine[at0:at0 + 32, 128 * q:128 * q + 128]

    def add2(first, last):
        def body(p):
            new = []
            for c in range(3):
                def lines_of(i):
                    return P21[pl.ds(pl.multiple_of((10 * c + i) * 24, 8), 24)]

                mid = 0.75 * lines_of(p)
                even = mid + 0.25 * lines_of(p - 1)
                odd = mid + 0.25 * lines_of(p + 1)
                new.append((V1B[c, 2 * p] + even) * (XM1[...] * ym1(2 * p)))
                new.append((V1B[c, 2 * p + 1] + odd) * (XM1[...] * ym1(2 * p + 1)))
            for c in range(3):
                V1B[c, 2 * p] = new[2 * c]
                V1B[c, 2 * p + 1] = new[2 * c + 1]

        loop(first, last, body)

    def spread1(first, last):
        for c in range(3):
            CZ[c] = split_dot(V1B[c, 4:16].reshape(288, 128), M10[...]).reshape(12, 24, 128)

        def body(p):
            lines = []
            for b in range(2):
                for c in range(3):
                    a = 0.75 * CZ[c, p] + 0.25 * CZ[c, p - 1 + 2 * b]
                    mid = 0.75 * roll(a, -4, 0)
                    lines.append((mid + 0.25 * roll(a, -3, 0), mid + 0.25 * roll(a, -5, 0)))
            slot = lax.rem(p, 4)
            for k in range(6):
                TMP[slot, k, pl.ds(0, 16, stride=2)] = lines[k][0][0:16]
                TMP[slot, k, pl.ds(1, 16, stride=2)] = lines[k][1][0:16]
            new = []
            for b in range(2):
                y = 2 * p - 1 + b
                m = XM0[...] * ym0(y)
                for c in range(3):
                    new.append((VB[c, y] + TMP[slot, 3 * b + c]) * m)
            for b in range(2):
                for c in range(3):
                    VB[c, 2 * p - 1 + b] = new[3 * b + c]

        loop(first, last, body)

    for cycle in range(2):
        if cycle == 0:
            far_in = []
            planes(4, 18, start0, store0)
            sweep0(VA, VB, 5, 17)
        else:
            sweep0(VB, VA, 4, 18)
            sweep0(VA, VB, 5, 17)
        residue0(VB)
        source1(cycle)
        s1 = RS1.at[cycle]
        s1_near = [box_copy(s1, s1, peer) for peer in NEAR]
        sent += s1_near

        if cycle == 0:
            received(a2_x)
            rows = []
            for f in range(6):
                one = XA[pl.ds(2 * f, 8, stride=16)]
                two = XA[pl.ds(2 * f + 1, 8, stride=16)]
                A2[f, 8] = one
                A2[f, 9] = two
                rows.append(one + two)
            RA3[192:208] = pack(split_dot(jnp.concatenate(rows, axis=0), P23[...]), 4)
            a2_y = [
                send(A2.at[:, 8:10], A2.at[:, pl.ds(8 - 2 * d * side, 2)], (d * side, 0)) for d in (2, 1)
            ]
            chip = pl.ds(jnp.clip(gx - core - 1, 0, 4), 4)
            a2_y.append(
                send(A2.at[:, 8:10, chip], A2.at[:, pl.ds(8 - 6 * side, 2), chip], (3 * side, 0))
            )
            a2_y.append(
                send(
                    A2.at[:, pl.ds(9 - core, 1), chip],
                    A2.at[:, pl.ds(9 - core - 8 * side, 1), chip],
                    (4 * side, 0),
                )
            )
            a3_y = [
                send(RA3.at[192:204], RA3.at[pl.ds(pl.multiple_of(16 * (12 - d * side), 16), 12)], (d * side, 0))
                for d in range(1, 12)
            ]
            sent += a2_y + a3_y
            received(a1_near)
            loop(1, 4, functools.partial(unpack, RA1, A1, low6))
            loop(4, 16, inverse1)

        received(s1_near)
        loop(1, 4, functools.partial(unpack, s1, S1, low4))
        loop(5, 15, start1)
        sweep1(V1A, V1B, 6, 14)
        residue1(V1B)
        source2(cycle)
        own = pl.ds(pl.multiple_of(gx * 8, 8), 8)
        s2 = []
        for dy, dx in SHEET:
            first, size = {2: (3, 3), -2: (0, 3)}.get(dy, (0, 6))
            rows = pl.ds(pl.multiple_of(gx * 8, 8) + first, size)
            s2.append(send(XG.at[cycle, 2, rows], XG.at[cycle, 2 - dy, rows], (dy, dx)))
        sent += s2
        s1_far = [outer_copy(s1, peer, cycle) for peer in OUTER]
        sent += s1_far
        if cycle == 0:
            a1_far = [outer_copy(RA1, peer, cycle) for peer in OUTER]
            sent += a1_far
            received(a2_y)
            a2_swap = pl.ds(1 + 9 * core, 7)
            a2_y = [send(A2.at[:, a2_swap], A2.at[:, a2_swap], twin)]
            received(a3_y)
            a3_swap = pl.ds(pl.multiple_of(16 + 192 * core, 16), 176)
            a3_y = [send(RA3.at[a3_swap], RA3.at[a3_swap], twin)]
            sent += a2_y + a3_y
            received(a2_y)
            m = damped_inverse([A2[f] for f in range(6)], W[2], YM2[...])
            for f in range(6):
                I2[f] = m[f]
        received(s2)
        for i in range(5):
            for c in range(3):
                for j in range(2):
                    if (i, j) not in ((0, 0), (4, 1)):
                        S2[cycle, c, 4 + 2 * i + j] = XG[cycle, i, pl.ds(3 * j + c, 8, stride=8)]
        start2(cycle, 5, 13)
        sweep2(cycle, V2A, V2B, 6, 12)
        source3(cycle)
        reach = [d for d in RING if abs(d) <= 11 - cycle]
        s3 = [send(SG.at[cycle, 96:102], SG.at[cycle, 96 - 8 * d:102 - 8 * d], (d, 0)) for d in reach]

        s2_far = []
        beside = pl.ds(jnp.clip(gx - 1, 0, 5), 3)
        for d in (3, -3, 2, -2, 4, -4):
            if abs(d) == 3:
                first, size = 8, 2
            else:
                first, size = (8 if d in (2, -4) else 9), 1
            if abs(d) < 4 or cycle == 0:
                s2_far.append(
                    send(
                        S2.at[cycle, :, first:first + size, beside],
                        S2.at[cycle, :, first - 2 * d:first - 2 * d + size, beside],
                        (d, 0),
                    )
                )
        if cycle == 0:
            for dy in (1, -1):
                far_in.append(input_copy((dy, 0), y_far[dy], (0, 8, 16)))
            for dy in (1, -1):
                for dx in (1, -1):
                    far_in.append(input_copy((dy, dx), y_far[dy], x_some[dx]))
                    far_in.append(input_copy((dy, dx), y_near[dy], x_rest[dx]))
            sent += far_in
            received(a3_y)
            place = iota((24, 128), 0) + (gy - 12)
            mask = jnp.where((place >= 0) & (place < 32), 1.0, 0.0)
            for h in range(2):
                m = damped_inverse([RA3[pl.ds(2 * f + h, 24, stride=16)] for f in range(6)], W[3], mask)
                for f in range(6):
                    I3[f, h] = m[f]
        received(s1_far)
        for group in (0, 4):
            unpack(s1, S1, low4, group)
        if cycle == 1:
            loop(3, 5, start1)
            loop(15, 17, start1)
            sweep1(V1A, V1B, 4, 6)
            sweep1(V1A, V1B, 14, 16)
            for copy in sent:
                copy.wait_send()
        received(s2_far)
        start2(cycle, 1, 5)
        start2(cycle, 13, 17)
        sweep2(cycle, V2A, V2B, 2, 6)
        sweep2(cycle, V2A, V2B, 12, 16)
        late = s3 + s2_far
        if cycle == 0:
            sent += late

        received(s3)
        solve3(cycle)
        spread3()
        sweep2(cycle, V2B, V2A, 3, 15)
        sweep2(cycle, V2A, V2B, 4, 14)
        spread2()
        if cycle == 0:
            received(a1_far)
            for group in (0, 4):
                unpack(RA1, A1, low6, group)
            loop(0, 4, inverse1)
            loop(16, 20, inverse1)
            loop(1, 5, start1)
            loop(15, 19, start1)
            sweep1(V1A, V1B, 2, 6)
            sweep1(V1A, V1B, 14, 18)
            add2(1, 9)
            sweep1(V1B, V1A, 3, 17)
            sweep1(V1A, V1B, 4, 16)
            received(far_in)
            planes(0, 8, start0, store0)
            planes(14, 22, start0, store0)
            sweep0(VA, VB, 1, 9)
            sweep0(VA, VB, 13, 21)
            spread1(1, 11)
            sweep0(VB, VA, 2, 20)
            sweep0(VA, VB, 3, 19)
        else:
            add2(2, 8)
            sweep1(V1B, V1A, 5, 15)
            sweep1(V1A, V1B, 6, 14)
            spread1(3, 9)
            sweep0(VB, VA, 6, 16)

            def last(y, new):
                for c in range(3):
                    out[c, y - 7] = new[c][8:24]

            planes(7, 15, functools.partial(swept0, VA), last)
            for copy in late:
                copy.wait_send()


TRANSFERS = 220


def local(spatial_grad, temporal_grad):
    def v(*shape, dtype=F32):
        return pltpu.VMEM(shape, dtype)

    def m(*shape):
        return pltpu.VMEM(shape, BF16)

    scratch = [
        v(4, 22, 32, 128), v(22, 32, 128), v(3, 22, 32, 128), v(3, 22, 32, 128), v(3, 10, 32, 128),
        v(32, 128), v(6, 32, 128), v(3, 12, 24, 128), v(4, 6, 32, 128),
        v(5, 3, 6, 2, 8, 128), v(6, 20, 24, 128), v(6, 20, 24, 128), v(2, 5, 3, 3, 2, 8, 128), v(3, 20, 24, 128),
        v(3, 20, 24, 128), v(3, 20, 24, 128), v(3, 6, 24, 128), v(24, 128),
        v(192, 128), v(192, 128), v(128, 128), v(128, 128), v(6, 18, 8, 128), v(6, 18, 8, 128), v(2, 5, 64, 128),
        v(2, 3, 18, 8, 128), v(3, 18, 8, 128), v(3, 18, 8, 128), v(18, 8, 128), v(2, 272, 128), v(768, 128),
        v(384, 128), v(6, 2, 24, 128), v(2, 192, 128), v(3, 2, 24, 128), v(2, 96, 128), v(384, 128),
        m(128, 128), m(128, 128), m(128, 128), m(128, 128), m(128, 128), m(128, 128),
        m(2, 128, 512), m(128, 512), m(128, 128),
        pltpu.SemaphoreType.DMA((2,)),
        pltpu.SemaphoreType.DMA((TRANSFERS,)),
        pltpu.SemaphoreType.DMA((TRANSFERS,)),
    ]
    return pl.pallas_call(
        kernel,
        out_shape=jax.ShapeDtypeStruct(spatial_grad.shape, F32),
        in_specs=[pl.BlockSpec(memory_space=pl.ANY)] * 2,
        out_specs=pl.BlockSpec(memory_space=pltpu.VMEM),
        scratch_shapes=scratch,
        compiler_params=pltpu.CompilerParams(
            collective_id=0, has_side_effects=True, vmem_limit_bytes=60 * 2**20
        ),
        name="flow",
    )(spatial_grad, temporal_grad)


def solution(mesh):
    placed = (P(None, "gy", "gx", None), P("gy", "gx", None))
    return jax.shard_map(
        local, mesh=mesh, in_specs=placed, out_specs=P(None, "gy", "gx", None), check_vma=False
    )
```

```python
import functools

import jax
import jax.numpy as jnp
from jax import lax
from jax.experimental import pallas as pl
from jax.experimental.pallas import tpu as pltpu
from jax.sharding import PartitionSpec as P

MESH = pl.DeviceIdType.MESH
F32 = jnp.float32
BF16 = jnp.bfloat16
GROUP = 2
UNROLL = 16
KEEP = 0.2
DAMP = 0.8
W = (1.0, 0.25, 0.0625, 0.015625)

NEAR = [(a, b) for a in (-1, 0, 1) for b in (-1, 0, 1) if (a, b) != (0, 0)]
OUTER = [(a, b) for a in (-2, 2) for b in (-1, 0, 1)]
BOX = NEAR + OUTER
SHEET = [(a, b) for a in (2, -2, 1, -1, 0) for b in (4, 3, 5, 2, 6, 1, 7, 0) if (a, b) != (0, 0)]
RING = [s * d for d in (11, 4, 5, 3, 10, 6, 2, 9, 7, 1, 8) for s in (1, -1)]


def loop(first, last, body):
    def step(i, carry):
        body(i)
        return carry

    lax.fori_loop(first, last, step, 0, unroll=min(UNROLL, last - first))


def planes(first, last, compute, store):
    def body(i):
        y = first + GROUP * i
        new = [compute(y + k) for k in range(GROUP)]
        for k in range(GROUP):
            store(y + k, new[k])

    assert (last - first) % GROUP == 0
    loop(0, (last - first) // GROUP, body)


def iota(shape, dim):
    return lax.broadcasted_iota(jnp.int32, shape, dim)


def roll(x, shift, axis):
    return pltpu.roll(x, shift % x.shape[axis], axis)


def split_dot(x, matrix):
    high = x.astype(BF16).astype(F32)
    both = jnp.concatenate([high, x - high], axis=0).astype(BF16)
    out = jnp.dot(both, matrix, preferred_element_type=F32)
    rows = x.shape[0]
    return out[:rows] + out[rows:]


def fold_weight(d):
    return jnp.where((d == 0) | (d == 1), 3.0, jnp.where((d == -1) | (d == 2), 1.0, 0.0))


def spread_weight(d):
    return jnp.where((d == 0) | (d == 1), 0.75, jnp.where((d == -1) | (d == 2), 0.25, 0.0))


def sym(m, v):
    return [
        m[0] * v[0] + m[3] * v[1] + m[4] * v[2],
        m[3] * v[0] + m[1] * v[1] + m[5] * v[2],
        m[4] * v[0] + m[5] * v[1] + m[2] * v[2],
    ]


def damped_inverse(m, weight, mask):
    dx, dy, dz = (m[k] + 6.0 * weight for k in range(3))
    xy, xz, yz = m[3], m[4], m[5]
    cof = [
        dy * dz - yz * yz,
        dx * dz - xz * xz,
        dx * dy - xy * xy,
        xz * yz - xy * dz,
        xy * yz - dy * xz,
        xy * xz - dx * yz,
    ]
    det = dx * cof[0] + xy * cof[3] + xz * cof[4]
    scale = mask * DAMP / det
    return [c * scale for c in cof]


def kernel(
    sg, tg, out,
    IN, Q, VA, VB, R0, XM0, FS, CZ, TMP,
    RA1, A1, I1, RS1, S1, V1A, V1B, R1, XM1,
    C1, C2, F, XA, A2, I2, XG, S2, V2A, V2B, YM2, E21, P21,
    RA3, I3, SG, V3, E3, P3,
    M01, M12, M23, P01, P12, P23, M32, M21, M10,
    lsem, ssem, rsem,
):
    gy = lax.axis_index("gy")
    gx = lax.axis_index("gx")

    load_g = pltpu.make_async_copy(sg, IN.at[0:3, 7:15, 8:24], lsem.at[0])
    load_t = pltpu.make_async_copy(tg, IN.at[3, 7:15, 8:24], lsem.at[1])
    load_g.start()
    load_t.start()

    core = lax.rem(gx, 2)
    side = 1 - 2 * core
    twin = (0, side)

    def at(dy, dx):
        return lax.rem(gy + dy + 32, 32), lax.rem(gx + dx + 8, 8)

    S2[...] = jnp.zeros_like(S2)
    A2[...] = jnp.zeros_like(A2)
    SG[...] = jnp.zeros_like(SG)
    RA3[...] = jnp.zeros_like(RA3)
    barrier = pltpu.get_barrier_semaphore()
    everyone = SHEET + [(d, 0) for d in RING if abs(d) > 2]
    for peer in everyone:
        pl.semaphore_signal(barrier, inc=1, device_id=at(*peer), device_id_type=MESH)

    count = [0]

    def send(src, dst, peer):
        k = count[0]
        count[0] += 1
        copy = pltpu.make_async_remote_copy(
            src_ref=src, dst_ref=dst, send_sem=ssem.at[k], recv_sem=rsem.at[k],
            device_id=at(*peer), device_id_type=MESH,
        )
        copy.start()
        return copy

    def received(copies):
        for copy in copies:
            copy.wait_recv()

    sent = []

    load_g.wait()
    load_t.wait()
    pl.semaphore_wait(barrier, len(everyone))

    def input_copy(peer, rows, columns):
        (y0, y1, height), (x0, x1, width) = rows, columns
        return send(
            IN.at[:, 7 + y0:7 + y0 + height, 8 + x0:8 + x0 + width],
            IN.at[:, y1:y1 + height, x1:x1 + width],
            peer,
        )

    y_near = {1: (5, 4, 3), -1: (0, 15, 3)}
    y_far = {1: (1, 0, 4), -1: (3, 18, 4)}
    y_mid = {1: (3, 2, 2), -1: (3, 18, 2)}
    y_end = {1: (1, 0, 2), -1: (5, 20, 2)}
    x_near = {1: (13, 5, 3), -1: (0, 24, 3)}
    x_some = {1: (12, 4, 4), -1: (0, 24, 4)}
    x_rest = {1: (9, 1, 4), -1: (3, 27, 4)}
    x_all = {1: (8, 0, 8), -1: (0, 24, 8)}

    near_in = [input_copy((dy, dx), y_near[dy], x_near[dx]) for dy in (1, -1) for dx in (1, -1)]
    near_in += [input_copy((dy, 0), y_near[dy], (0, 8, 16)) for dy in (1, -1)]
    near_in += [input_copy((0, dx), (0, 7, 8), x_all[dx]) for dx in (1, -1)]
    def lanes(shape):
        return iota(shape, 0), iota(shape, 1)

    k, n = lanes((128, 128))
    M01[...] = (fold_weight(k - 2 * (n & 63)) * (1.0 / 512.0)).astype(BF16)
    P01[...] = jnp.where((k >> 1) == (n & 63), 0.125, 0.0).astype(BF16)
    M12[...] = jnp.where(k < 64, fold_weight(k - 2 * (n & 31)) * (1.0 / 512.0), 0.0).astype(BF16)
    P12[...] = jnp.where((k < 64) & ((k >> 1) == (n & 31)), 0.125, 0.0).astype(BF16)
    part = (n & 31) >> 4
    M23[...] = jnp.where(
        (k >> 5) == 2 * part, fold_weight((k & 31) - 2 * (n & 15)) * (1.0 / 512.0), 0.0
    ).astype(BF16)
    P23[...] = jnp.where(((k >> 6) == part) & (((k & 31) >> 1) == (n & 15)), 0.125, 0.0).astype(BF16)
    M10[...] = jnp.where(k < 64, spread_weight(n - 2 * k), 0.0).astype(BF16)
    for q in range(4):
        M21[:, 128 * q:128 * q + 128] = jnp.where(
            ((k >> 5) == q) & (n < 64), spread_weight(n - 2 * (k & 31)), 0.0
        ).astype(BF16)
        for eo in range(2):
            xs = n >> 5
            fits = ((xs & 1) == eo) & ((k >> 4) == 2 * q + (xs >> 1))
            M32[eo, :, 128 * q:128 * q + 128] = jnp.where(
                fits, spread_weight((n & 31) - 2 * (k & 15)), 0.0
            ).astype(BF16)

    row = iota((32, 128), 0) + (16 * gx - 8)
    XM0[...] = jnp.where((row >= 0) & (row < 128), 1.0, 0.0)
    row = iota((24, 128), 0) + (8 * gx - 8)
    XM1[...] = jnp.where((row >= 0) & (row < 64) & (iota((24, 128), 1) < 64), 1.0, 0.0)
    plane = iota((18, 8, 128), 0) + (2 * gy - 8)
    YM2[...] = jnp.where((plane >= 0) & (plane < 64), 1.0, 0.0)
    E21[...] = jnp.zeros_like(E21)

    def ym(first, length, y):
        place = first + y
        return jnp.where((place >= 0) & (place < length), 1.0, 0.0).astype(F32)

    def ym0(y):
        return ym(8 * gy - 7, 256, y)

    def ym1(y):
        return ym(4 * gy - 8, 128, y)

    def pack(rows, group):
        size = rows.shape[0]
        keep = (iota(rows.shape, 1) >> 5) == (iota(rows.shape, 0) & 3)
        F[0:size] = jnp.where(keep, rows, 0.0)
        kept = 8 * ((size // group + 7) // 8)
        total = F[pl.ds(0, kept, stride=group)]
        for r in range(1, group):
            total = total + F[pl.ds(r, kept, stride=group)]
        return total

    F[...] = jnp.zeros_like(F)

    def own_coeffs(i):
        def products(y):
            g = [IN[c, y, 8:24] for c in range(3)]
            return [g[0] * g[0], g[1] * g[1], g[2] * g[2], g[0] * g[1], g[0] * g[2], g[1] * g[2]]

        one, two = products(7 + 2 * i), products(8 + 2 * i)
        for f in range(6):
            FS[f, 0:16] = one[f] + two[f]
        for f in range(6):
            C1[pl.ds(f * 32 + 8 * i, 8)] = FS[f, pl.ds(0, 8, stride=2)] + FS[f, pl.ds(1, 8, stride=2)]

    loop(0, 4, own_coeffs)
    C2[...] = split_dot(C1[...], P01[...])
    low = iota((8, 128), 1) < 64
    for f in range(6):
        for j in range(2):
            RA1[2, 1, f, j] = jnp.where(
                low, C2[32 * f + 8 * j:32 * f + 8 * j + 8], C2[32 * f + 8 * j + 16:32 * f + 8 * j + 24]
            )
    halved = C2[pl.ds(0, 96, stride=2)] + C2[pl.ds(1, 96, stride=2)]
    XA[pl.ds(pl.multiple_of(gx * 16, 16), 16)] = pack(split_dot(halved, P12[...]), 8)

    own_a2 = pl.ds(pl.multiple_of(gx * 16, 16), 16)
    a2_x = [send(XA.at[own_a2], XA.at[own_a2], (0, d)) for d in range(1, 8)]

    def box_copy(src, dst, peer):
        return send(src.at[2, 1], dst.at[2 - peer[0], 1 - peer[1]], peer)

    def outer_copy(buf, peer, cycle):
        dy, dx = peer
        rows = slice(0, 2) if cycle == 0 else (slice(1, 2) if dy > 0 else slice(0, 1))
        wide = 3 if cycle == 0 else 1
        columns = {1: slice(8 - wide, 8), 0: slice(0, 8), -1: slice(0, wide)}[dx]
        return send(buf.at[2, 1, :, rows, columns], buf.at[2 - dy, 1 - dx, :, rows, columns], peer)

    a1_near = [box_copy(RA1, RA1, peer) for peer in NEAR]
    sent += near_in + a2_x + a1_near
    received(near_in)

    lane0 = iota((32, 128), 1)
    first_lane, last_lane = lane0 == 0, lane0 == 127

    def around0(src, y):
        centre, total = [], []
        for c in range(3):
            v = src[c, y]
            n = src[c, y - 1] + src[c, y + 1]
            n = n + (roll(v, 1, 0) + roll(v, -1, 0))
            n = n + jnp.where(first_lane, 0.0, roll(v, 1, 1)) + jnp.where(last_lane, 0.0, roll(v, -1, 1))
            centre.append(v)
            total.append(n)
        return centre, total

    def dot3(a, b):
        return a[0] * b[0] + a[1] * b[1] + a[2] * b[2]

    def start0(y):
        g = [IN[c, y] for c in range(3)]
        q = XM0[...] * ym0(y) * (DAMP / 6.0) / (6.0 + dot3(g, g))
        scale = -6.0 * IN[3, y] * q
        return q, [scale * g[c] for c in range(3)]

    def store0(y, new):
        Q[y] = new[0]
        for c in range(3):
            VA[c, y] = new[1][c]

    def swept0(src, y):
        g = [IN[c, y] for c in range(3)]
        t = IN[3, y]
        v, n = around0(src, y)
        p = [n[c] - t * g[c] for c in range(3)]
        d = dot3(g, p) * Q[y]
        scale = XM0[...] * (ym0(y) * (DAMP / 6.0))
        return [KEEP * v[c] + scale * p[c] - d * g[c] for c in range(3)]

    def sweep0(src, dst, first, last):
        def store(y, new):
            for c in range(3):
                dst[c, y] = new[c]

        planes(first, last, functools.partial(swept0, src), store)

    def residue0(src):
        def compute(y):
            g = [IN[c, y] for c in range(3)]
            v, n = around0(src, y)
            d = IN[3, y] + dot3(g, v)
            m = XM0[...] * ym0(y)
            return [m * (n[c] - 6.0 * v[c] - g[c] * d) for c in range(3)]

        def store(y, new):
            for c in range(3):
                R0[c, y - 6] = new[c]

        planes(6, 16, compute, store)

    def fold_rows(src, c, y, x, size):
        weights = (1.0, 3.0, 3.0, 1.0)
        total = None
        for kx in range(4):
            line = None
            for ky in range(4):
                term = src[c, y + ky, pl.ds(x + kx, size, stride=2)]
                term = term if weights[ky] == 1.0 else weights[ky] * term
                line = term if line is None else line + term
            line = line if weights[kx] == 1.0 else weights[kx] * line
            total = line if total is None else total + line
        return total

    def source1(cycle):
        lines = [fold_rows(R0, c, 2 * i, 7, 8) for c in range(3) for i in range(4)]
        s = split_dot(jnp.concatenate(lines, axis=0), M01[...])
        for c in range(3):
            for j in range(2):
                at0 = 32 * c + 8 * j
                RS1[cycle, 2, 1, c, j] = jnp.where(low, s[at0:at0 + 8], s[at0 + 16:at0 + 24])

    low4 = iota((3, 2, 8, 128), 3) < 64
    low6 = iota((6, 2, 8, 128), 3) < 64

    def unpack(src, dst, mask, group):
        for dx in range(3):
            p = src[group, dx]
            other = pltpu.roll(p.reshape(-1, 128), 64, 1).reshape(p.shape)
            dst[:, pl.ds(4 * group, 2), 8 * dx:8 * dx + 8] = jnp.where(mask, p, 0.0)
            dst[:, pl.ds(4 * group + 2, 2), 8 * dx:8 * dx + 8] = jnp.where(mask, other, 0.0)

    def inverse1(y):
        m = damped_inverse([A1[f, y] for f in range(6)], W[1], XM1[...] * ym1(y))
        for f in range(6):
            I1[f, y] = m[f]

    def around1(src, y):
        centre, total = [], []
        for c in range(3):
            v = src[c, y]
            n = src[c, y - 1] + src[c, y + 1]
            n = n + (roll(v, 1, 0) + roll(v, -1, 0)) + (roll(v, 1, 1) + roll(v, -1, 1))
            centre.append(v)
            total.append(n)
        return centre, total

    def start1(y):
        new = sym([I1[f, y] for f in range(6)], [S1[c, y] for c in range(3)])
        for c in range(3):
            V1A[c, y] = new[c]

    def sweep1(src, dst, first, last):
        def compute(y):
            v, n = around1(src, y)
            new = sym([I1[f, y] for f in range(6)], [S1[c, y] + W[1] * n[c] for c in range(3)])
            return [KEEP * v[c] + new[c] for c in range(3)]

        def store(y, new):
            for c in range(3):
                dst[c, y] = new[c]

        planes(first, last, compute, store)

    def residue1(src):
        def compute(y):
            v, n = around1(src, y)
            av = sym([A1[f, y] for f in range(6)], v)
            m = XM1[...] * ym1(y)
            return [m * (S1[c, y] + W[1] * (n[c] - 6.0 * v[c]) - av[c]) for c in range(3)]

        def store(y, new):
            for c in range(3):
                R1[c, y - 7] = new[c]

        planes(7, 13, compute, store)

    def source2(cycle):
        lines = [fold_rows(R1, c, 2 * i, 7, 4) for i in range(2) for c in range(3)]
        for k in range(6):
            FS[0, 4 * k:4 * k + 4] = lines[k]
        XG[cycle, 2, pl.ds(pl.multiple_of(gx * 8, 8), 8)] = pack(split_dot(FS[0, 0:24], M12[...]), 4)

    def shifts2(v):
        lane, r = iota(v.shape, 1), iota(v.shape, 0) & 7
        up = roll(v, -32, 1)
        xp = jnp.where(lane < 96, up, jnp.where(r == 7, 0.0, roll(up, -1, 0)))
        down = roll(v, 32, 1)
        xm = jnp.where(lane >= 32, down, jnp.where(r == 0, 0.0, roll(down, 1, 0)))
        return xm, xp

    def around2(src, first, last):
        centre, total = [], []
        for c in range(3):
            v3 = src[c, first:last]
            v = v3.reshape(-1, 128)
            z = iota(v.shape, 1) & 31
            xm, xp = shifts2(v)
            n = xm + xp + jnp.where(z == 0, 0.0, roll(v, 1, 1)) + jnp.where(z == 31, 0.0, roll(v, -1, 1))
            n = n.reshape(v3.shape) + (src[c, first - 1:last - 1] + src[c, first + 1:last + 1])
            centre.append(v3)
            total.append(n)
        return centre, total

    def start2(cycle, first, last):
        new = sym([I2[f, first:last] for f in range(6)], [S2[cycle, c, first:last] for c in range(3)])
        for c in range(3):
            V2A[c, first:last] = new[c]

    def sweep2(cycle, src, dst, first, last):
        v, n = around2(src, first, last)
        p = [S2[cycle, c, first:last] + W[2] * n[c] for c in range(3)]
        new = sym([I2[f, first:last] for f in range(6)], p)
        for c in range(3):
            dst[c, first:last] = KEEP * v[c] + new[c]

    def source3(cycle):
        v, n = around2(V2B, 7, 11)
        av = sym([A2[f, 7:11] for f in range(6)], v)
        rows = []
        for c in range(3):
            r = YM2[7:11] * (S2[cycle, c, 7:11] + W[2] * (n[c] - 6.0 * v[c]) - av[c])
            f = r[0] + 3.0 * (r[1] + r[2]) + r[3]
            xm, xp = shifts2(f)
            _, more = shifts2(3.0 * f + xp)
            rows.append(xm + 3.0 * f + more)
        SG[cycle, 96:104] = pack(split_dot(jnp.concatenate(rows, axis=0), M23[...]), 4)

    lane3 = iota((24, 128), 1)

    def shifts3(a, b):
        ua, ub = roll(a, -16, 1), roll(b, -16, 1)
        da, db = roll(a, 16, 1), roll(b, 16, 1)
        up = jnp.where(lane3 < 112, ua, ub), jnp.where(lane3 < 112, ub, 0.0)
        down = jnp.where(lane3 >= 16, da, 0.0), jnp.where(lane3 >= 16, db, da)
        return down, up

    def solve3(cycle):
        s = [[SG[cycle, pl.ds(2 * c + h, 24, stride=8)] for h in range(2)] for c in range(3)]
        for h in range(2):
            new = sym([I3[f, h] for f in range(6)], [s[c][h] for c in range(3)])
            for c in range(3):
                V3[c, h] = new[c]

        def body(i):
            v = [[V3[c, h] for h in range(2)] for c in range(3)]
            p = [[None, None] for c in range(3)]
            for c in range(3):
                down, up = shifts3(v[c][0], v[c][1])
                for h in range(2):
                    a = v[c][h]
                    n = roll(a, 1, 0) + roll(a, -1, 0) + down[h] + up[h]
                    n = n + jnp.where((lane3 & 15) == 0, 0.0, roll(a, 1, 1))
                    n = n + jnp.where((lane3 & 15) == 15, 0.0, roll(a, -1, 1))
                    p[c][h] = SG[cycle, pl.ds(2 * c + h, 24, stride=8)] + W[3] * n
            for h in range(2):
                new = sym([I3[f, h] for f in range(6)], [p[c][h] for c in range(3)])
                for c in range(3):
                    V3[c, h] = KEEP * v[c][h] + new[c]

        loop(0, 7, body)

    def spread3():
        for c in range(3):
            a, b = V3[c, 0], V3[c, 1]
            down, up = shifts3(a, b)
            for h, v in enumerate((a, b)):
                even = 0.75 * v + 0.25 * down[h]
                odd = 0.75 * v + 0.25 * up[h]
                E3[0, pl.ds(32 * c + h, 16, stride=2)] = even[8:24]
                E3[1, pl.ds(32 * c + h, 16, stride=2)] = odd[8:24]
        fine = split_dot(E3[0], M32[0]) + split_dot(E3[1], M32[1])
        for q in range(4):
            P3[pl.ds(q, 96, stride=4)] = fine[:, 128 * q:128 * q + 128]
        for c in range(3):
            def planes(i):
                return P3[128 * c + 8 * i:128 * c + 8 * i + 56].reshape(7, 8, 128)

            before, mid, after = planes(0), planes(1), planes(2)
            even = 0.75 * mid + 0.25 * before
            odd = 0.75 * mid + 0.25 * after
            for i in range(7):
                y = 2 + 2 * i
                V2B[c, y] = (V2B[c, y] + even[i]) * YM2[y]
                V2B[c, y + 1] = (V2B[c, y + 1] + odd[i]) * YM2[y + 1]

    def spread2():
        for c in range(3):
            v = V2B[c, 4:14].reshape(80, 128)
            xm, xp = shifts2(v)
            E21[0, 8 + 80 * c:88 + 80 * c] = 0.75 * v + 0.25 * xm
            E21[1, 8 + 80 * c:88 + 80 * c] = 0.75 * v + 0.25 * xp
        lines = []
        for j in range(3):
            inside = (gx + j >= 1) & (gx + j <= 8)
            for eo in range(2):
                lines.append(jnp.where(inside, E21[eo, pl.ds(7 + gx + j, 32, stride=8)], 0.0))
        fine = split_dot(jnp.concatenate(lines, axis=0), M21[...])
        for j in range(3):
            for eo in range(2):
                for q in range(4):
                    at0 = 32 * (2 * j + eo)
                    P21[pl.ds(8 * j + 2 * q + eo, 32, stride=24)] = fine[at0:at0 + 32, 128 * q:128 * q + 128]

    def add2(first, last):
        def body(p):
            new = []
            for c in range(3):
                def lines_of(i):
                    return P21[pl.ds(pl.multiple_of((10 * c + i) * 24, 8), 24)]

                mid = 0.75 * lines_of(p)
                even = mid + 0.25 * lines_of(p - 1)
                odd = mid + 0.25 * lines_of(p + 1)
                new.append((V1B[c, 2 * p] + even) * (XM1[...] * ym1(2 * p)))
                new.append((V1B[c, 2 * p + 1] + odd) * (XM1[...] * ym1(2 * p + 1)))
            for c in range(3):
                V1B[c, 2 * p] = new[2 * c]
                V1B[c, 2 * p + 1] = new[2 * c + 1]

        loop(first, last, body)

    def widen1():
        for c in range(3):
            CZ[c] = split_dot(V1B[c, 4:16].reshape(288, 128), M10[...]).reshape(12, 24, 128)

    def spread1(first, last):
        def body(p):
            lines = []
            for b in range(2):
                for c in range(3):
                    a = 0.75 * CZ[c, p] + 0.25 * CZ[c, p - 1 + 2 * b]
                    mid = 0.75 * roll(a, -4, 0)
                    lines.append((mid + 0.25 * roll(a, -3, 0), mid + 0.25 * roll(a, -5, 0)))
            slot = lax.rem(p, 4)
            for k in range(6):
                TMP[slot, k, pl.ds(0, 16, stride=2)] = lines[k][0][0:16]
                TMP[slot, k, pl.ds(1, 16, stride=2)] = lines[k][1][0:16]
            new = []
            for b in range(2):
                y = 2 * p - 1 + b
                m = XM0[...] * ym0(y)
                for c in range(3):
                    new.append((VB[c, y] + TMP[slot, 3 * b + c]) * m)
            for b in range(2):
                for c in range(3):
                    VB[c, 2 * p - 1 + b] = new[3 * b + c]

        loop(first, last, body)

    for cycle in range(2):
        if cycle == 0:
            far_in = [input_copy((dy, 0), y_mid[dy], (0, 8, 16)) for dy in (1, -1)]
            planes(4, 18, start0, store0)
            sweep0(VA, VB, 5, 17)
        else:
            sweep0(VB, VA, 4, 18)
            sweep0(VA, VB, 5, 17)
        residue0(VB)
        source1(cycle)
        s1 = RS1.at[cycle]
        s1_near = [box_copy(s1, s1, peer) for peer in NEAR]
        sent += s1_near

        if cycle == 0:
            received(a2_x)
            rows = []
            for f in range(6):
                one = XA[pl.ds(2 * f, 8, stride=16)]
                two = XA[pl.ds(2 * f + 1, 8, stride=16)]
                A2[f, 8] = one
                A2[f, 9] = two
                rows.append(one + two)
            RA3[192:208] = pack(split_dot(jnp.concatenate(rows, axis=0), P23[...]), 4)
            a2_y = [
                send(A2.at[:, 8:10], A2.at[:, pl.ds(8 - 2 * d * side, 2)], (d * side, 0)) for d in (2, 1)
            ]
            chip = pl.ds(jnp.clip(gx - core - 1, 0, 4), 4)
            a2_y.append(
                send(A2.at[:, 8:10, chip], A2.at[:, pl.ds(8 - 6 * side, 2), chip], (3 * side, 0))
            )
            a2_y.append(
                send(
                    A2.at[:, pl.ds(9 - core, 1), chip],
                    A2.at[:, pl.ds(9 - core - 8 * side, 1), chip],
                    (4 * side, 0),
                )
            )
            a3_y = [
                send(RA3.at[192:204], RA3.at[pl.ds(pl.multiple_of(16 * (12 - d * side), 16), 12)], (d * side, 0))
                for d in range(1, 12)
            ]
            sent += a2_y + a3_y
            received(a1_near)
            loop(1, 4, functools.partial(unpack, RA1, A1, low6))
            loop(4, 16, inverse1)

        received(s1_near)
        loop(1, 4, functools.partial(unpack, s1, S1, low4))
        loop(5, 15, start1)
        sweep1(V1A, V1B, 6, 14)
        residue1(V1B)
        source2(cycle)
        own = pl.ds(pl.multiple_of(gx * 8, 8), 8)
        s2 = []
        for dy, dx in SHEET:
            first, size = {2: (3, 3), -2: (0, 3)}.get(dy, (0, 6))
            rows = pl.ds(pl.multiple_of(gx * 8, 8) + first, size)
            s2.append(send(XG.at[cycle, 2, rows], XG.at[cycle, 2 - dy, rows], (dy, dx)))
        sent += s2
        s1_far = [outer_copy(s1, peer, cycle) for peer in OUTER]
        sent += s1_far
        if cycle == 0:
            a1_far = [outer_copy(RA1, peer, cycle) for peer in OUTER]
            sent += a1_far
            received(a2_y)
            a2_swap = pl.ds(1 + 9 * core, 7)
            a2_y = [send(A2.at[:, a2_swap], A2.at[:, a2_swap], twin)]
            received(a3_y)
            a3_swap = pl.ds(pl.multiple_of(16 + 192 * core, 16), 176)
            a3_y = [send(RA3.at[a3_swap], RA3.at[a3_swap], twin)]
            sent += a2_y + a3_y
            received(a2_y)
            m = damped_inverse([A2[f] for f in range(6)], W[2], YM2[...])
            for f in range(6):
                I2[f] = m[f]
        received(s2)
        for i in range(5):
            for c in range(3):
                for j in range(2):
                    if (i, j) not in ((0, 0), (4, 1)):
                        S2[cycle, c, 4 + 2 * i + j] = XG[cycle, i, pl.ds(3 * j + c, 8, stride=8)]
        start2(cycle, 5, 13)
        sweep2(cycle, V2A, V2B, 6, 12)
        source3(cycle)
        reach = [d for d in RING if abs(d) <= 11 - cycle]
        s3 = [send(SG.at[cycle, 96:102], SG.at[cycle, 96 - 8 * d:102 - 8 * d], (d, 0)) for d in reach]

        s2_far = []
        beside = pl.ds(jnp.clip(gx - 1, 0, 5), 3)
        for d in (3, -3, 2, -2, 4, -4):
            if abs(d) == 3:
                first, size = 8, 2
            else:
                first, size = (8 if d in (2, -4) else 9), 1
            if abs(d) < 4 or cycle == 0:
                s2_far.append(
                    send(
                        S2.at[cycle, :, first:first + size, beside],
                        S2.at[cycle, :, first - 2 * d:first - 2 * d + size, beside],
                        (d, 0),
                    )
                )
        if cycle == 0:
            for dy in (1, -1):
                far_in.append(input_copy((dy, 0), y_end[dy], (0, 8, 16)))
            for dy in (1, -1):
                for dx in (1, -1):
                    far_in.append(input_copy((dy, dx), y_far[dy], x_some[dx]))
                    far_in.append(input_copy((dy, dx), y_near[dy], x_rest[dx]))
            sent += far_in
            received(a3_y)
            place = iota((24, 128), 0) + (gy - 12)
            mask = jnp.where((place >= 0) & (place < 32), 1.0, 0.0)
            for h in range(2):
                m = damped_inverse([RA3[pl.ds(2 * f + h, 24, stride=16)] for f in range(6)], W[3], mask)
                for f in range(6):
                    I3[f, h] = m[f]
        received(s1_far)
        for group in (0, 4):
            unpack(s1, S1, low4, group)
        if cycle == 1:
            loop(3, 5, start1)
            loop(15, 17, start1)
            sweep1(V1A, V1B, 4, 6)
            sweep1(V1A, V1B, 14, 16)
            for copy in sent:
                copy.wait_send()
        late = s3 + s2_far
        if cycle == 0:
            sent += late

        received(s3)
        solve3(cycle)
        received(s2_far)
        start2(cycle, 1, 5)
        start2(cycle, 13, 17)
        sweep2(cycle, V2A, V2B, 2, 6)
        sweep2(cycle, V2A, V2B, 12, 16)
        spread3()
        sweep2(cycle, V2B, V2A, 3, 15)
        sweep2(cycle, V2A, V2B, 4, 14)
        spread2()
        if cycle == 0:
            received(a1_far)
            for group in (0, 4):
                unpack(RA1, A1, low6, group)
            loop(0, 4, inverse1)
            loop(16, 20, inverse1)
            loop(1, 5, start1)
            loop(15, 19, start1)
            sweep1(V1A, V1B, 2, 6)
            sweep1(V1A, V1B, 14, 18)
            add2(1, 9)
            sweep1(V1B, V1A, 3, 17)
            sweep1(V1A, V1B, 4, 16)
            widen1()
            received(far_in)
            planes(0, 8, start0, store0)
            planes(14, 22, start0, store0)
            sweep0(VA, VB, 1, 9)
            sweep0(VA, VB, 13, 21)
            spread1(1, 11)
            sweep0(VB, VA, 2, 20)
            sweep0(VA, VB, 3, 19)
        else:
            add2(2, 8)
            sweep1(V1B, V1A, 5, 15)
            sweep1(V1A, V1B, 6, 14)
            widen1()
            spread1(3, 9)
            sweep0(VB, VA, 6, 16)

            def last(y, new):
                for c in range(3):
                    out[c, y - 7] = new[c][8:24]

            planes(7, 15, functools.partial(swept0, VA), last)
            for copy in late:
                copy.wait_send()


TRANSFERS = 220


def local(spatial_grad, temporal_grad):
    def v(*shape, dtype=F32):
        return pltpu.VMEM(shape, dtype)

    def m(*shape):
        return pltpu.VMEM(shape, BF16)

    scratch = [
        v(4, 22, 32, 128), v(22, 32, 128), v(3, 22, 32, 128), v(3, 22, 32, 128), v(3, 10, 32, 128),
        v(32, 128), v(6, 32, 128), v(3, 12, 24, 128), v(4, 6, 32, 128),
        v(5, 3, 6, 2, 8, 128), v(6, 20, 24, 128), v(6, 20, 24, 128), v(2, 5, 3, 3, 2, 8, 128), v(3, 20, 24, 128),
        v(3, 20, 24, 128), v(3, 20, 24, 128), v(3, 6, 24, 128), v(24, 128),
        v(192, 128), v(192, 128), v(128, 128), v(128, 128), v(6, 18, 8, 128), v(6, 18, 8, 128), v(2, 5, 64, 128),
        v(2, 3, 18, 8, 128), v(3, 18, 8, 128), v(3, 18, 8, 128), v(18, 8, 128), v(2, 272, 128), v(768, 128),
        v(384, 128), v(6, 2, 24, 128), v(2, 192, 128), v(3, 2, 24, 128), v(2, 96, 128), v(384, 128),
        m(128, 128), m(128, 128), m(128, 128), m(128, 128), m(128, 128), m(128, 128),
        m(2, 128, 512), m(128, 512), m(128, 128),
        pltpu.SemaphoreType.DMA((2,)),
        pltpu.SemaphoreType.DMA((TRANSFERS,)),
        pltpu.SemaphoreType.DMA((TRANSFERS,)),
    ]
    return pl.pallas_call(
        kernel,
        out_shape=pltpu.VMEM(spatial_grad.shape, F32),
        in_specs=[pl.BlockSpec(memory_space=pl.ANY)] * 2,
        out_specs=pl.BlockSpec(memory_space=pltpu.VMEM),
        scratch_shapes=scratch,
        compiler_params=pltpu.CompilerParams(
            collective_id=0, has_side_effects=True, vmem_limit_bytes=56 * 2**20
        ),
        name="flow",
    )(spatial_grad, temporal_grad)


def solution(mesh):
    placed = (P(None, "gy", "gx", None), P("gy", "gx", None))
    return jax.shard_map(
        local, mesh=mesh, in_specs=placed, out_specs=P(None, "gy", "gx", None), check_vma=False
    )
```

```python
import functools

import jax
import jax.numpy as jnp
from jax import lax
from jax.experimental import pallas as pl
from jax.experimental.pallas import tpu as pltpu
from jax.sharding import PartitionSpec as P

MESH = pl.DeviceIdType.MESH
F32 = jnp.float32
BF16 = jnp.bfloat16
GROUP = 2
UNROLL = 16
KEEP = 0.2
DAMP = 0.8
W = (1.0, 0.25, 0.0625, 0.015625)

NEAR = [(a, b) for a in (-1, 0, 1) for b in (-1, 0, 1) if (a, b) != (0, 0)]
OUTER = [(a, b) for a in (-2, 2) for b in (-1, 0, 1)]
BOX = NEAR + OUTER
SHEET = [(a, b) for a in (2, -2, 1, -1, 0) for b in (4, 3, 5, 2, 6, 1, 7, 0) if (a, b) != (0, 0)]
RING = [s * d for d in (11, 4, 5, 3, 10, 6, 2, 9, 7, 1, 8) for s in (1, -1)]


def loop(first, last, body):
    def step(i, carry):
        body(i)
        return carry

    lax.fori_loop(first, last, step, 0, unroll=min(UNROLL, last - first))


def planes(first, last, compute, store):
    def body(i):
        y = first + GROUP * i
        new = [compute(y + k) for k in range(GROUP)]
        for k in range(GROUP):
            store(y + k, new[k])

    assert (last - first) % GROUP == 0
    loop(0, (last - first) // GROUP, body)


def iota(shape, dim):
    return lax.broadcasted_iota(jnp.int32, shape, dim)


def roll(x, shift, axis):
    return pltpu.roll(x, shift % x.shape[axis], axis)


def split_dot(x, matrix):
    high = x.astype(BF16).astype(F32)
    both = jnp.concatenate([high, x - high], axis=0).astype(BF16)
    out = jnp.dot(both, matrix, preferred_element_type=F32)
    rows = x.shape[0]
    return out[:rows] + out[rows:]


def fold_weight(d):
    return jnp.where((d == 0) | (d == 1), 3.0, jnp.where((d == -1) | (d == 2), 1.0, 0.0))


def spread_weight(d):
    return jnp.where((d == 0) | (d == 1), 0.75, jnp.where((d == -1) | (d == 2), 0.25, 0.0))


def sym(m, v):
    return [
        m[0] * v[0] + m[3] * v[1] + m[4] * v[2],
        m[3] * v[0] + m[1] * v[1] + m[5] * v[2],
        m[4] * v[0] + m[5] * v[1] + m[2] * v[2],
    ]


def damped_inverse(m, weight, mask):
    dx, dy, dz = (m[k] + 6.0 * weight for k in range(3))
    xy, xz, yz = m[3], m[4], m[5]
    cof = [
        dy * dz - yz * yz,
        dx * dz - xz * xz,
        dx * dy - xy * xy,
        xz * yz - xy * dz,
        xy * yz - dy * xz,
        xy * xz - dx * yz,
    ]
    det = dx * cof[0] + xy * cof[3] + xz * cof[4]
    scale = mask * DAMP / det
    return [c * scale for c in cof]


def kernel(
    sg, tg, out,
    IN, Q, VA, VB, R0, XM0, FS, CZ, TMP,
    RA1, A1, I1, RS1, S1, V1A, V1B, R1, XM1,
    C1, C2, F, XA, A2, I2, XG, S2, V2A, V2B, YM2, E21, P21,
    RA3, I3, SG, V3, E3, P3,
    M01, M12, M23, P01, P12, P23, M32, M21, M10,
    lsem, ssem, rsem,
):
    gy = lax.axis_index("gy")
    gx = lax.axis_index("gx")

    load_g = pltpu.make_async_copy(sg, IN.at[0:3, 7:15, 8:24], lsem.at[0])
    load_t = pltpu.make_async_copy(tg, IN.at[3, 7:15, 8:24], lsem.at[1])
    load_g.start()
    load_t.start()

    core = lax.rem(gx, 2)
    side = 1 - 2 * core
    twin = (0, side)

    def at(dy, dx):
        return lax.rem(gy + dy + 32, 32), lax.rem(gx + dx + 8, 8)

    S2[...] = jnp.zeros_like(S2)
    A2[...] = jnp.zeros_like(A2)
    SG[...] = jnp.zeros_like(SG)
    RA3[...] = jnp.zeros_like(RA3)
    barrier = pltpu.get_barrier_semaphore()
    everyone = [(d, 0) for d in RING if abs(d) > 2] + SHEET
    for peer in everyone:
        pl.semaphore_signal(barrier, inc=1, device_id=at(*peer), device_id_type=MESH)

    count = [0]

    def send(src, dst, peer):
        k = count[0]
        count[0] += 1
        copy = pltpu.make_async_remote_copy(
            src_ref=src, dst_ref=dst, send_sem=ssem.at[k], recv_sem=rsem.at[k],
            device_id=at(*peer), device_id_type=MESH,
        )
        copy.start()
        return copy

    def received(copies):
        for copy in copies:
            copy.wait_recv()

    sent = []

    load_g.wait()
    load_t.wait()
    pl.semaphore_wait(barrier, len(everyone))

    def input_copy(peer, rows, columns):
        (y0, y1, height), (x0, x1, width) = rows, columns
        return send(
            IN.at[:, 7 + y0:7 + y0 + height, 8 + x0:8 + x0 + width],
            IN.at[:, y1:y1 + height, x1:x1 + width],
            peer,
        )

    y_near = {1: (5, 4, 3), -1: (0, 15, 3)}
    y_far = {1: (1, 0, 4), -1: (3, 18, 4)}
    y_mid = {1: (3, 2, 2), -1: (3, 18, 2)}
    y_end = {1: (1, 0, 2), -1: (5, 20, 2)}
    x_near = {1: (13, 5, 3), -1: (0, 24, 3)}
    x_some = {1: (12, 4, 4), -1: (0, 24, 4)}
    x_rest = {1: (9, 1, 4), -1: (3, 27, 4)}
    x_all = {1: (8, 0, 8), -1: (0, 24, 8)}

    near_in = [input_copy((dy, dx), y_near[dy], x_near[dx]) for dy in (1, -1) for dx in (1, -1)]
    near_in += [input_copy((dy, 0), y_near[dy], (0, 8, 16)) for dy in (1, -1)]
    near_in += [input_copy((0, dx), (0, 7, 8), x_all[dx]) for dx in (1, -1)]
    def lanes(shape):
        return iota(shape, 0), iota(shape, 1)

    k, n = lanes((128, 128))
    M01[...] = (fold_weight(k - 2 * (n & 63)) * (1.0 / 512.0)).astype(BF16)
    P01[...] = jnp.where((k >> 1) == (n & 63), 0.125, 0.0).astype(BF16)
    M12[...] = jnp.where(k < 64, fold_weight(k - 2 * (n & 31)) * (1.0 / 512.0), 0.0).astype(BF16)
    P12[...] = jnp.where((k < 64) & ((k >> 1) == (n & 31)), 0.125, 0.0).astype(BF16)
    part = (n & 31) >> 4
    M23[...] = jnp.where(
        (k >> 5) == 2 * part, fold_weight((k & 31) - 2 * (n & 15)) * (1.0 / 512.0), 0.0
    ).astype(BF16)
    P23[...] = jnp.where(((k >> 6) == part) & (((k & 31) >> 1) == (n & 15)), 0.125, 0.0).astype(BF16)
    M10[...] = jnp.where(k < 64, spread_weight(n - 2 * k), 0.0).astype(BF16)
    for q in range(4):
        M21[:, 128 * q:128 * q + 128] = jnp.where(
            ((k >> 5) == q) & (n < 64), spread_weight(n - 2 * (k & 31)), 0.0
        ).astype(BF16)
        for eo in range(2):
            xs = n >> 5
            fits = ((xs & 1) == eo) & ((k >> 4) == 2 * q + (xs >> 1))
            M32[eo, :, 128 * q:128 * q + 128] = jnp.where(
                fits, spread_weight((n & 31) - 2 * (k & 15)), 0.0
            ).astype(BF16)

    row = iota((32, 128), 0) + (16 * gx - 8)
    XM0[...] = jnp.where((row >= 0) & (row < 128), 1.0, 0.0)
    row = iota((24, 128), 0) + (8 * gx - 8)
    XM1[...] = jnp.where((row >= 0) & (row < 64) & (iota((24, 128), 1) < 64), 1.0, 0.0)
    plane = iota((18, 8, 128), 0) + (2 * gy - 8)
    YM2[...] = jnp.where((plane >= 0) & (plane < 64), 1.0, 0.0)
    E21[...] = jnp.zeros_like(E21)

    def ym(first, length, y):
        place = first + y
        return jnp.where((place >= 0) & (place < length), 1.0, 0.0).astype(F32)

    def ym0(y):
        return ym(8 * gy - 7, 256, y)

    def ym1(y):
        return ym(4 * gy - 8, 128, y)

    def pack(rows, group):
        size = rows.shape[0]
        keep = (iota(rows.shape, 1) >> 5) == (iota(rows.shape, 0) & 3)
        F[0:size] = jnp.where(keep, rows, 0.0)
        kept = 8 * ((size // group + 7) // 8)
        total = F[pl.ds(0, kept, stride=group)]
        for r in range(1, group):
            total = total + F[pl.ds(r, kept, stride=group)]
        return total

    F[...] = jnp.zeros_like(F)

    def own_coeffs(i):
        def products(y):
            g = [IN[c, y, 8:24] for c in range(3)]
            return [g[0] * g[0], g[1] * g[1], g[2] * g[2], g[0] * g[1], g[0] * g[2], g[1] * g[2]]

        one, two = products(7 + 2 * i), products(8 + 2 * i)
        for f in range(6):
            FS[f, 0:16] = one[f] + two[f]
        for f in range(6):
            C1[pl.ds(f * 32 + 8 * i, 8)] = FS[f, pl.ds(0, 8, stride=2)] + FS[f, pl.ds(1, 8, stride=2)]

    loop(0, 4, own_coeffs)
    C2[...] = split_dot(C1[...], P01[...])
    low = iota((8, 128), 1) < 64
    for f in range(6):
        for j in range(2):
            RA1[2, 1, f, j] = jnp.where(
                low, C2[32 * f + 8 * j:32 * f + 8 * j + 8], C2[32 * f + 8 * j + 16:32 * f + 8 * j + 24]
            )
    halved = C2[pl.ds(0, 96, stride=2)] + C2[pl.ds(1, 96, stride=2)]
    XA[pl.ds(pl.multiple_of(gx * 16, 16), 16)] = pack(split_dot(halved, P12[...]), 8)

    own_a2 = pl.ds(pl.multiple_of(gx * 16, 16), 16)
    a2_x = [send(XA.at[own_a2], XA.at[own_a2], (0, d)) for d in range(1, 8)]

    def box_copy(src, dst, peer):
        return send(src.at[2, 1], dst.at[2 - peer[0], 1 - peer[1]], peer)

    def outer_copy(buf, peer, cycle):
        dy, dx = peer
        rows = slice(0, 2) if cycle == 0 else (slice(1, 2) if dy > 0 else slice(0, 1))
        wide = 3 if cycle == 0 else 1
        columns = {1: slice(8 - wide, 8), 0: slice(0, 8), -1: slice(0, wide)}[dx]
        return send(buf.at[2, 1, :, rows, columns], buf.at[2 - dy, 1 - dx, :, rows, columns], peer)

    a1_near = [box_copy(RA1, RA1, peer) for peer in NEAR]
    sent += near_in + a2_x + a1_near
    received(near_in)

    lane0 = iota((32, 128), 1)
    first_lane, last_lane = lane0 == 0, lane0 == 127

    def around0(src, y):
        centre, total = [], []
        for c in range(3):
            v = src[c, y]
            n = src[c, y - 1] + src[c, y + 1]
            n = n + (roll(v, 1, 0) + roll(v, -1, 0))
            n = n + jnp.where(first_lane, 0.0, roll(v, 1, 1)) + jnp.where(last_lane, 0.0, roll(v, -1, 1))
            centre.append(v)
            total.append(n)
        return centre, total

    def dot3(a, b):
        return a[0] * b[0] + a[1] * b[1] + a[2] * b[2]

    def start0(y):
        g = [IN[c, y] for c in range(3)]
        q = XM0[...] * ym0(y) * (DAMP / 6.0) / (6.0 + dot3(g, g))
        scale = -6.0 * IN[3, y] * q
        return q, [scale * g[c] for c in range(3)]

    def store0(y, new):
        Q[y] = new[0]
        for c in range(3):
            VA[c, y] = new[1][c]

    def swept0(src, y, own=slice(0, 32)):
        g = [IN[c, y, own] for c in range(3)]
        t = IN[3, y, own]
        v, n = around0(src, y)
        v, n = [a[own] for a in v], [a[own] for a in n]
        p = [n[c] - t * g[c] for c in range(3)]
        d = dot3(g, p) * Q[y, own]
        scale = XM0[own] * (ym0(y) * (DAMP / 6.0))
        return [KEEP * v[c] + scale * p[c] - d * g[c] for c in range(3)]

    def sweep0(src, dst, first, last):
        def store(y, new):
            for c in range(3):
                dst[c, y] = new[c]

        planes(first, last, functools.partial(swept0, src), store)

    def residue0(src):
        def compute(y):
            g = [IN[c, y] for c in range(3)]
            v, n = around0(src, y)
            d = IN[3, y] + dot3(g, v)
            m = XM0[...] * ym0(y)
            return [m * (n[c] - 6.0 * v[c] - g[c] * d) for c in range(3)]

        def store(y, new):
            for c in range(3):
                R0[c, y - 6] = new[c]

        planes(6, 16, compute, store)

    def fold_rows(src, c, y, x, size):
        weights = (1.0, 3.0, 3.0, 1.0)
        total = None
        for kx in range(4):
            line = None
            for ky in range(4):
                term = src[c, y + ky, pl.ds(x + kx, size, stride=2)]
                term = term if weights[ky] == 1.0 else weights[ky] * term
                line = term if line is None else line + term
            line = line if weights[kx] == 1.0 else weights[kx] * line
            total = line if total is None else total + line
        return total

    def source1(cycle):
        lines = [fold_rows(R0, c, 2 * i, 7, 8) for c in range(3) for i in range(4)]
        s = split_dot(jnp.concatenate(lines, axis=0), M01[...])
        for c in range(3):
            for j in range(2):
                at0 = 32 * c + 8 * j
                RS1[cycle, 2, 1, c, j] = jnp.where(low, s[at0:at0 + 8], s[at0 + 16:at0 + 24])

    low4 = iota((3, 2, 8, 128), 3) < 64
    low6 = iota((6, 2, 8, 128), 3) < 64

    def unpack(src, dst, mask, group):
        for dx in range(3):
            p = src[group, dx]
            other = pltpu.roll(p.reshape(-1, 128), 64, 1).reshape(p.shape)
            dst[:, pl.ds(4 * group, 2), 8 * dx:8 * dx + 8] = jnp.where(mask, p, 0.0)
            dst[:, pl.ds(4 * group + 2, 2), 8 * dx:8 * dx + 8] = jnp.where(mask, other, 0.0)

    def inverse1(y):
        m = damped_inverse([A1[f, y] for f in range(6)], W[1], XM1[...] * ym1(y))
        for f in range(6):
            I1[f, y] = m[f]

    def around1(src, y):
        centre, total = [], []
        for c in range(3):
            v = src[c, y]
            n = src[c, y - 1] + src[c, y + 1]
            n = n + (roll(v, 1, 0) + roll(v, -1, 0)) + (roll(v, 1, 1) + roll(v, -1, 1))
            centre.append(v)
            total.append(n)
        return centre, total

    def start1(y):
        new = sym([I1[f, y] for f in range(6)], [S1[c, y] for c in range(3)])
        for c in range(3):
            V1A[c, y] = new[c]

    def sweep1(src, dst, first, last):
        def compute(y):
            v, n = around1(src, y)
            new = sym([I1[f, y] for f in range(6)], [S1[c, y] + W[1] * n[c] for c in range(3)])
            return [KEEP * v[c] + new[c] for c in range(3)]

        def store(y, new):
            for c in range(3):
                dst[c, y] = new[c]

        planes(first, last, compute, store)

    def residue1(src):
        def compute(y):
            v, n = around1(src, y)
            av = sym([A1[f, y] for f in range(6)], v)
            m = XM1[...] * ym1(y)
            return [m * (S1[c, y] + W[1] * (n[c] - 6.0 * v[c]) - av[c]) for c in range(3)]

        def store(y, new):
            for c in range(3):
                R1[c, y - 7] = new[c]

        planes(7, 13, compute, store)

    def source2(cycle):
        lines = [fold_rows(R1, c, 2 * i, 7, 4) for i in range(2) for c in range(3)]
        for k in range(6):
            FS[0, 4 * k:4 * k + 4] = lines[k]
        XG[cycle, 2, pl.ds(pl.multiple_of(gx * 8, 8), 8)] = pack(split_dot(FS[0, 0:24], M12[...]), 4)

    def shifts2(v):
        lane, r = iota(v.shape, 1), iota(v.shape, 0) & 7
        up = roll(v, -32, 1)
        xp = jnp.where(lane < 96, up, jnp.where(r == 7, 0.0, roll(up, -1, 0)))
        down = roll(v, 32, 1)
        xm = jnp.where(lane >= 32, down, jnp.where(r == 0, 0.0, roll(down, 1, 0)))
        return xm, xp

    def around2(src, first, last):
        centre, total = [], []
        for c in range(3):
            v3 = src[c, first:last]
            v = v3.reshape(-1, 128)
            z = iota(v.shape, 1) & 31
            xm, xp = shifts2(v)
            n = xm + xp + jnp.where(z == 0, 0.0, roll(v, 1, 1)) + jnp.where(z == 31, 0.0, roll(v, -1, 1))
            n = n.reshape(v3.shape) + (src[c, first - 1:last - 1] + src[c, first + 1:last + 1])
            centre.append(v3)
            total.append(n)
        return centre, total

    def start2(cycle, first, last):
        new = sym([I2[f, first:last] for f in range(6)], [S2[cycle, c, first:last] for c in range(3)])
        for c in range(3):
            V2A[c, first:last] = new[c]

    def sweep2(cycle, src, dst, first, last):
        v, n = around2(src, first, last)
        p = [S2[cycle, c, first:last] + W[2] * n[c] for c in range(3)]
        new = sym([I2[f, first:last] for f in range(6)], p)
        for c in range(3):
            dst[c, first:last] = KEEP * v[c] + new[c]

    def source3(cycle):
        v, n = around2(V2B, 7, 11)
        av = sym([A2[f, 7:11] for f in range(6)], v)
        rows = []
        for c in range(3):
            r = YM2[7:11] * (S2[cycle, c, 7:11] + W[2] * (n[c] - 6.0 * v[c]) - av[c])
            f = r[0] + 3.0 * (r[1] + r[2]) + r[3]
            xm, xp = shifts2(f)
            _, more = shifts2(3.0 * f + xp)
            rows.append(xm + 3.0 * f + more)
        SG[cycle, 96:104] = pack(split_dot(jnp.concatenate(rows, axis=0), M23[...]), 4)

    lane3 = iota((24, 128), 1)

    def shifts3(a, b):
        ua, ub = roll(a, -16, 1), roll(b, -16, 1)
        da, db = roll(a, 16, 1), roll(b, 16, 1)
        up = jnp.where(lane3 < 112, ua, ub), jnp.where(lane3 < 112, ub, 0.0)
        down = jnp.where(lane3 >= 16, da, 0.0), jnp.where(lane3 >= 16, db, da)
        return down, up

    def solve3(cycle):
        s = [[SG[cycle, pl.ds(2 * c + h, 24, stride=8)] for h in range(2)] for c in range(3)]
        for h in range(2):
            new = sym([I3[f, h] for f in range(6)], [s[c][h] for c in range(3)])
            for c in range(3):
                V3[c, h] = new[c]

        def body(i):
            v = [[V3[c, h] for h in range(2)] for c in range(3)]
            p = [[None, None] for c in range(3)]
            for c in range(3):
                down, up = shifts3(v[c][0], v[c][1])
                for h in range(2):
                    a = v[c][h]
                    n = roll(a, 1, 0) + roll(a, -1, 0) + down[h] + up[h]
                    n = n + jnp.where((lane3 & 15) == 0, 0.0, roll(a, 1, 1))
                    n = n + jnp.where((lane3 & 15) == 15, 0.0, roll(a, -1, 1))
                    p[c][h] = SG[cycle, pl.ds(2 * c + h, 24, stride=8)] + W[3] * n
            for h in range(2):
                new = sym([I3[f, h] for f in range(6)], [p[c][h] for c in range(3)])
                for c in range(3):
                    V3[c, h] = KEEP * v[c][h] + new[c]

        loop(0, 7, body)

    def spread3():
        for c in range(3):
            a, b = V3[c, 0], V3[c, 1]
            down, up = shifts3(a, b)
            for h, v in enumerate((a, b)):
                even = 0.75 * v + 0.25 * down[h]
                odd = 0.75 * v + 0.25 * up[h]
                E3[0, pl.ds(32 * c + h, 16, stride=2)] = even[8:24]
                E3[1, pl.ds(32 * c + h, 16, stride=2)] = odd[8:24]
        fine = split_dot(E3[0], M32[0]) + split_dot(E3[1], M32[1])
        for q in range(4):
            P3[pl.ds(q, 96, stride=4)] = fine[:, 128 * q:128 * q + 128]
        for c in range(3):
            def planes(i):
                return P3[128 * c + 8 * i:128 * c + 8 * i + 56].reshape(7, 8, 128)

            before, mid, after = planes(0), planes(1), planes(2)
            even = 0.75 * mid + 0.25 * before
            odd = 0.75 * mid + 0.25 * after
            for i in range(7):
                y = 2 + 2 * i
                V2B[c, y] = (V2B[c, y] + even[i]) * YM2[y]
                V2B[c, y + 1] = (V2B[c, y + 1] + odd[i]) * YM2[y + 1]

    def spread2():
        for c in range(3):
            v = V2B[c, 4:14].reshape(80, 128)
            xm, xp = shifts2(v)
            E21[0, 8 + 80 * c:88 + 80 * c] = 0.75 * v + 0.25 * xm
            E21[1, 8 + 80 * c:88 + 80 * c] = 0.75 * v + 0.25 * xp
        lines = []
        for j in range(3):
            inside = (gx + j >= 1) & (gx + j <= 8)
            for eo in range(2):
                lines.append(jnp.where(inside, E21[eo, pl.ds(7 + gx + j, 32, stride=8)], 0.0))
        fine = split_dot(jnp.concatenate(lines, axis=0), M21[...])
        for j in range(3):
            for eo in range(2):
                for q in range(4):
                    at0 = 32 * (2 * j + eo)
                    P21[pl.ds(8 * j + 2 * q + eo, 32, stride=24)] = fine[at0:at0 + 32, 128 * q:128 * q + 128]

    def add2(first, last):
        def body(p):
            new = []
            for c in range(3):
                def lines_of(i):
                    return P21[pl.ds(pl.multiple_of((10 * c + i) * 24, 8), 24)]

                mid = 0.75 * lines_of(p)
                even = mid + 0.25 * lines_of(p - 1)
                odd = mid + 0.25 * lines_of(p + 1)
                new.append((V1B[c, 2 * p] + even) * (XM1[...] * ym1(2 * p)))
                new.append((V1B[c, 2 * p + 1] + odd) * (XM1[...] * ym1(2 * p + 1)))
            for c in range(3):
                V1B[c, 2 * p] = new[2 * c]
                V1B[c, 2 * p + 1] = new[2 * c + 1]

        loop(first, last, body)

    def widen1(first, last):
        for c in range(3):
            lines = V1B[c, 4 + first:4 + last].reshape(-1, 128)
            CZ[c, first:last] = split_dot(lines, M10[...]).reshape(last - first, 24, 128)

    def spread1(first, last):
        def body(p):
            lines = []
            for b in range(2):
                for c in range(3):
                    a = 0.75 * CZ[c, p] + 0.25 * CZ[c, p - 1 + 2 * b]
                    mid = 0.75 * roll(a, -4, 0)
                    lines.append((mid + 0.25 * roll(a, -3, 0), mid + 0.25 * roll(a, -5, 0)))
            slot = lax.rem(p, 4)
            for k in range(6):
                TMP[slot, k, pl.ds(0, 16, stride=2)] = lines[k][0][0:16]
                TMP[slot, k, pl.ds(1, 16, stride=2)] = lines[k][1][0:16]
            new = []
            for b in range(2):
                y = 2 * p - 1 + b
                m = XM0[...] * ym0(y)
                for c in range(3):
                    new.append((VB[c, y] + TMP[slot, 3 * b + c]) * m)
            for b in range(2):
                for c in range(3):
                    VB[c, 2 * p - 1 + b] = new[3 * b + c]

        loop(first, last, body)

    for cycle in range(2):
        if cycle == 0:
            far_in = [input_copy((dy, 0), y_mid[dy], (0, 8, 16)) for dy in (1, -1)]
            planes(4, 18, start0, store0)
            sweep0(VA, VB, 5, 17)
        else:
            sweep0(VB, VA, 4, 18)
            sweep0(VA, VB, 5, 17)
        residue0(VB)
        source1(cycle)
        s1 = RS1.at[cycle]
        s1_near = [box_copy(s1, s1, peer) for peer in NEAR]
        sent += s1_near

        if cycle == 0:
            received(a2_x)
            rows = []
            for f in range(6):
                one = XA[pl.ds(2 * f, 8, stride=16)]
                two = XA[pl.ds(2 * f + 1, 8, stride=16)]
                A2[f, 8] = one
                A2[f, 9] = two
                rows.append(one + two)
            RA3[192:208] = pack(split_dot(jnp.concatenate(rows, axis=0), P23[...]), 4)
            a2_y = [
                send(A2.at[:, 8:10], A2.at[:, pl.ds(8 - 2 * d * side, 2)], (d * side, 0)) for d in (2, 1)
            ]
            chip = pl.ds(jnp.clip(gx - core - 1, 0, 4), 4)
            a2_y.append(
                send(A2.at[:, 8:10, chip], A2.at[:, pl.ds(8 - 6 * side, 2), chip], (3 * side, 0))
            )
            a2_y.append(
                send(
                    A2.at[:, pl.ds(9 - core, 1), chip],
                    A2.at[:, pl.ds(9 - core - 8 * side, 1), chip],
                    (4 * side, 0),
                )
            )
            a3_y = [
                send(RA3.at[192:204], RA3.at[pl.ds(pl.multiple_of(16 * (12 - d * side), 16), 12)], (d * side, 0))
                for d in range(1, 12)
            ]
            sent += a2_y + a3_y
            received(a1_near)
            loop(1, 4, functools.partial(unpack, RA1, A1, low6))
            loop(4, 16, inverse1)

        received(s1_near)
        loop(1, 4, functools.partial(unpack, s1, S1, low4))
        loop(5, 15, start1)
        sweep1(V1A, V1B, 6, 14)
        residue1(V1B)
        source2(cycle)
        own = pl.ds(pl.multiple_of(gx * 8, 8), 8)
        s2 = []
        for dy, dx in SHEET:
            first, size = {2: (3, 3), -2: (0, 3)}.get(dy, (0, 6))
            rows = pl.ds(pl.multiple_of(gx * 8, 8) + first, size)
            s2.append(send(XG.at[cycle, 2, rows], XG.at[cycle, 2 - dy, rows], (dy, dx)))
        sent += s2
        s1_far = [outer_copy(s1, peer, cycle) for peer in OUTER]
        sent += s1_far
        if cycle == 0:
            a1_far = [outer_copy(RA1, peer, cycle) for peer in OUTER]
            sent += a1_far
            received(a2_y)
            a2_swap = pl.ds(1 + 9 * core, 7)
            a2_y = [send(A2.at[:, a2_swap], A2.at[:, a2_swap], twin)]
            received(a3_y)
            a3_swap = pl.ds(pl.multiple_of(16 + 192 * core, 16), 176)
            a3_y = [send(RA3.at[a3_swap], RA3.at[a3_swap], twin)]
            sent += a2_y + a3_y
            received(a2_y)
            m = damped_inverse([A2[f] for f in range(6)], W[2], YM2[...])
            for f in range(6):
                I2[f] = m[f]
        received(s2)
        for i in range(5):
            for c in range(3):
                for j in range(2):
                    if (i, j) not in ((0, 0), (4, 1)):
                        S2[cycle, c, 4 + 2 * i + j] = XG[cycle, i, pl.ds(3 * j + c, 8, stride=8)]
        start2(cycle, 5, 13)
        sweep2(cycle, V2A, V2B, 6, 12)
        source3(cycle)
        reach = [d for d in RING if abs(d) <= 11 - cycle]
        s3 = [send(SG.at[cycle, 96:102], SG.at[cycle, 96 - 8 * d:102 - 8 * d], (d, 0)) for d in reach]

        s2_far = []
        beside = pl.ds(jnp.clip(gx - 1, 0, 5), 3)
        for d in (3, -3, 2, -2, 4, -4):
            if abs(d) == 3:
                first, size = 8, 2
            else:
                first, size = (8 if d in (2, -4) else 9), 1
            if abs(d) < 4 or cycle == 0:
                s2_far.append(
                    send(
                        S2.at[cycle, :, first:first + size, beside],
                        S2.at[cycle, :, first - 2 * d:first - 2 * d + size, beside],
                        (d, 0),
                    )
                )
        if cycle == 0:
            for dy in (1, -1):
                for dx in (1, -1):
                    far_in.append(input_copy((dy, dx), y_far[dy], x_some[dx]))
                    far_in.append(input_copy((dy, dx), y_near[dy], x_rest[dx]))
            for dy in (1, -1):
                far_in.append(input_copy((dy, 0), y_end[dy], (0, 8, 16)))
            sent += far_in
            received(a3_y)
            place = iota((24, 128), 0) + (gy - 12)
            mask = jnp.where((place >= 0) & (place < 32), 1.0, 0.0)
            for h in range(2):
                m = damped_inverse([RA3[pl.ds(2 * f + h, 24, stride=16)] for f in range(6)], W[3], mask)
                for f in range(6):
                    I3[f, h] = m[f]
        received(s1_far)
        for group in (0, 4):
            unpack(s1, S1, low4, group)
        if cycle == 0:
            received(a1_far)
            for group in (0, 4):
                unpack(RA1, A1, low6, group)
            loop(0, 4, inverse1)
            loop(16, 20, inverse1)
            loop(1, 5, start1)
            loop(15, 19, start1)
            sweep1(V1A, V1B, 2, 6)
            sweep1(V1A, V1B, 14, 18)
        else:
            loop(3, 5, start1)
            loop(15, 17, start1)
            sweep1(V1A, V1B, 4, 6)
            sweep1(V1A, V1B, 14, 16)
        sent += s3 + s2_far
        if cycle == 1:
            for copy in sent:
                copy.wait_send()

        received(s3)
        solve3(cycle)
        received(s2_far)
        start2(cycle, 1 + cycle, 5)
        start2(cycle, 13, 17 - cycle)
        sweep2(cycle, V2A, V2B, 2 + cycle, 6)
        sweep2(cycle, V2A, V2B, 12, 16 - cycle)
        spread3()
        sweep2(cycle, V2B, V2A, 3 + cycle, 15 - cycle)
        sweep2(cycle, V2A, V2B, 4 + cycle, 14 - cycle)
        spread2()
        if cycle == 0:
            add2(1, 9)
            sweep1(V1B, V1A, 3, 17)
            sweep1(V1A, V1B, 4, 16)
            widen1(0, 12)
            received(far_in)
            planes(0, 8, start0, store0)
            planes(14, 22, start0, store0)
            sweep0(VA, VB, 1, 9)
            sweep0(VA, VB, 13, 21)
            spread1(1, 11)
            sweep0(VB, VA, 2, 20)
            sweep0(VA, VB, 3, 19)
        else:
            add2(2, 8)
            sweep1(V1B, V1A, 5, 15)
            sweep1(V1A, V1B, 6, 14)
            widen1(2, 10)
            spread1(3, 9)
            sweep0(VB, VA, 6, 16)

            def last(y, new):
                for c in range(3):
                    out[c, y - 7] = new[c]

            planes(7, 15, functools.partial(swept0, VA, own=slice(8, 24)), last)


TRANSFERS = 220


def local(spatial_grad, temporal_grad):
    def v(*shape, dtype=F32):
        return pltpu.VMEM(shape, dtype)

    def m(*shape):
        return pltpu.VMEM(shape, BF16)

    scratch = [
        v(4, 22, 32, 128), v(22, 32, 128), v(3, 22, 32, 128), v(3, 22, 32, 128), v(3, 10, 32, 128),
        v(32, 128), v(6, 32, 128), v(3, 12, 24, 128), v(4, 6, 32, 128),
        v(5, 3, 6, 2, 8, 128), v(6, 20, 24, 128), v(6, 20, 24, 128), v(2, 5, 3, 3, 2, 8, 128), v(3, 20, 24, 128),
        v(3, 20, 24, 128), v(3, 20, 24, 128), v(3, 6, 24, 128), v(24, 128),
        v(192, 128), v(192, 128), v(128, 128), v(128, 128), v(6, 18, 8, 128), v(6, 18, 8, 128), v(2, 5, 64, 128),
        v(2, 3, 18, 8, 128), v(3, 18, 8, 128), v(3, 18, 8, 128), v(18, 8, 128), v(2, 272, 128), v(768, 128),
        v(384, 128), v(6, 2, 24, 128), v(2, 192, 128), v(3, 2, 24, 128), v(2, 96, 128), v(384, 128),
        m(128, 128), m(128, 128), m(128, 128), m(128, 128), m(128, 128), m(128, 128),
        m(2, 128, 512), m(128, 512), m(128, 128),
        pltpu.SemaphoreType.DMA((2,)),
        pltpu.SemaphoreType.DMA((TRANSFERS,)),
        pltpu.SemaphoreType.DMA((TRANSFERS,)),
    ]
    return pl.pallas_call(
        kernel,
        out_shape=pltpu.VMEM(spatial_grad.shape, F32),
        in_specs=[pl.BlockSpec(memory_space=pl.ANY)] * 2,
        out_specs=pl.BlockSpec(memory_space=pltpu.VMEM),
        scratch_shapes=scratch,
        compiler_params=pltpu.CompilerParams(
            collective_id=0, has_side_effects=True, vmem_limit_bytes=56 * 2**20
        ),
        name="flow",
    )(spatial_grad, temporal_grad)


def solution(mesh):
    placed = (P(None, "gy", "gx", None), P("gy", "gx", None))
    return jax.shard_map(
        local, mesh=mesh, in_specs=placed, out_specs=P(None, "gy", "gx", None), check_vma=False
    )
```
